128 devices in a mesh: by: 8 (over y, core), bx: 16 (over z, x).
Axes of the slice: x: 4, y: 4, z: 4, core: 2. Of those that a mesh axis runs over, the one named last changes fastest.
Arguments:
- fields: float32 [3, 8, 2048, 4096], P(None, None, 'by', 'bx'), may hold values from -6 to 6
- level_count: int32 [2048, 4096], P('by', 'bx'), may hold values from 0 to 8, as said below
- thickness: float32 [8], replicated, may hold values from 0.05 to 0.3
- old_pressure: float32 [2048, 4096], P('by', 'bx'), may hold values from -6 to 6
Outputs:
- pressure: float32 [2048, 4096], P('by', 'bx')
- residual: float32 [2048, 4096], P('by', 'bx')
The draws below stay inside these ranges and needn't reach their ends.
Inputs may be any that keep to these rules, and one draw needn't show every extreme that they name: `level_count`: land comes in aligned squares of 8 x 8 cells, except that the cell at row 1, column 0 is always ocean with all 8 levels.
All inputs are finite; a program needn't handle non-finite values.
Results may differ from the reference program's by a relative error of at most 0.00024.
Values sent between devices are 32-bit elements; how exact they have to be, the bound alone decides.
A program may use at most 128 MiB of HBM per device.

```python
import math
import jax
import jax.numpy as jnp
from jax import lax

KM = 8
ITERS = 4
NX = 4096
NY = 2048


def draw_level_count(key, part):
    key_land = jax.random.fold_in(key, 11)
    key_levels = jax.random.fold_in(key, 23)
    coarse = jax.random.randint(key_land, (NY // 8, NX // 8), 0, 100)
    land = jnp.repeat(jnp.repeat(coarse < 30, 8, axis=0), 8, axis=1)
    levels = jax.random.randint(key_levels, (NY, NX), 1, KM + 1)
    counts = jnp.where(land, 0, levels)
    counts = counts.at[1, 0].set(KM)
    return counts.astype(jnp.int32)


def level_of(own_key, shape, cuts, least, top_value):
    def one(dim, parts):
        steps = jax.random.uniform(jax.random.fold_in(jax.random.fold_in(own_key, 6), dim), (parts,), jnp.float32, least / len(cuts), top_value / len(cuts))
        return jnp.repeat(jnp.exp(steps), shape[dim] // parts).reshape((-1,) + (1,) * (len(shape) - dim - 1))

    gain = one(*cuts[0])
    for cut in cuts[1:]:
        gain = gain * one(*cut)
    return gain


def normal_values(key, dims, spread, reach, shards=(), kind=jnp.bfloat16):
    drawn = jax.random.normal(key, dims, jnp.float32) * spread
    if len(shards) > 0:
        drawn = level_of(key, dims, shards, -0.22, 0.18) * drawn
    return jnp.clip(drawn, min=-reach, max=reach).astype(kind)


def setup_inputs(seed: int = 0) -> dict:
    key_of = jax.random.split(jax.random.key(seed), 5)
    fields = normal_values(key_of[0], (3, KM, NY, NX), 1.0, 6.0, ((2, 8), (3, 16)), jnp.float32)
    level_count = draw_level_count(jax.random.fold_in(key_of[4], 71), 0)
    thickness = jnp.clip(jnp.exp(jax.random.uniform(key_of[2], (KM,), jnp.float32, math.log(0.05), math.log(0.3))), 0.05, 0.3)
    old_pressure = normal_values(key_of[3], (NY, NX), 1.0, 6.0, ((0, 8), (1, 16)), jnp.float32)
    return {"fields": fields, "level_count": level_count, "thickness": thickness, "old_pressure": old_pressure}


VISCOSITY = 0.05
IMPLICIT = 0.05


def laplace(field):
    return (field[..., 1:-1, 2:] + field[..., 1:-1, :-2] + field[..., 2:, 1:-1]
            + field[..., :-2, 1:-1] - 4.0 * field[..., 1:-1, 1:-1])


def level_divergence(extended):
    zonal = extended[0]
    meridional = extended[1]
    baroclinic = extended[2]
    tend_zonal = -VISCOSITY * laplace(laplace(zonal)) - 0.5 * (baroclinic[..., 2:-2, 3:-1] - baroclinic[..., 2:-2, 1:-3])
    tend_merid = -VISCOSITY * laplace(laplace(meridional)) - 0.5 * (baroclinic[..., 3:-1, 2:-2] - baroclinic[..., 1:-3, 2:-2])
    return (0.5 * (tend_zonal[..., 1:-1, 2:] - tend_zonal[..., 1:-1, :-2])
            + 0.5 * (tend_merid[..., 2:, 1:-1] - tend_merid[..., :-2, 1:-1]))


def corner_min(extended_depth):
    return jnp.minimum(jnp.minimum(extended_depth[:-1, :-1], extended_depth[:-1, 1:]),
                       jnp.minimum(extended_depth[1:, :-1], extended_depth[1:, 1:]))


def operate(extended, corner):
    west_south = extended[:-1, :-1]
    east_south = extended[:-1, 1:]
    west_north = extended[1:, :-1]
    east_north = extended[1:, 1:]
    east_slope = 0.5 * (east_south + east_north - west_south - west_north)
    north_slope = 0.5 * (west_north + east_north - west_south - east_south)
    plus_flux = 0.5 * corner * (east_slope + north_slope)
    minus_flux = 0.5 * corner * (east_slope - north_slope)
    return (IMPLICIT * extended[1:-1, 1:-1] + plus_flux[:-1, :-1] - plus_flux[1:, 1:]
            + minus_flux[1:, :-1] - minus_flux[:-1, 1:])


def wrap_pad(field):
    return jnp.pad(field, 1, mode="wrap")


def reference(fields, level_count, thickness, old_pressure):
    def level_body(level, carry):
        total, depth_sum = carry
        layer = lax.dynamic_index_in_dim(fields, level, axis=1, keepdims=False)
        padded = jnp.pad(layer, ((0, 0), (3, 3), (3, 3)), mode="wrap")
        wet_mask = (level < level_count).astype(jnp.float32)
        weight = thickness[level] * wet_mask
        return total + weight * level_divergence(padded), depth_sum + weight

    zeros_field = jnp.zeros(old_pressure.shape, jnp.float32)
    forcing_sum, column_depth = lax.fori_loop(0, KM, level_body, (zeros_field, zeros_field))
    ocean_mask = (level_count > 0).astype(jnp.float32)
    right_side = ocean_mask * (forcing_sum + IMPLICIT * old_pressure)
    pressure = ocean_mask * old_pressure
    corner = corner_min(wrap_pad(column_depth))
    diagonal = IMPLICIT + 0.5 * (corner[1:, 1:] + corner[1:, :-1] + corner[:-1, 1:] + corner[:-1, :-1])
    residual = right_side - operate(wrap_pad(pressure), corner)
    precond = residual / diagonal
    direction = precond
    norm_now = jnp.sum(residual * precond)
    for iteration in range(ITERS):
        image_field = operate(wrap_pad(direction), corner)
        step_length = norm_now / jnp.sum(direction * image_field)
        pressure = pressure + step_length * direction
        residual = residual - step_length * image_field
        precond = residual / diagonal
        norm_next = jnp.sum(residual * precond)
        direction = precond + (norm_next / norm_now) * direction
        norm_now = norm_next
    return pressure, residual
```

```python
import functools

import jax
import jax.numpy as jnp
from jax import lax
from jax.experimental import pallas as pl
from jax.experimental.pallas import tpu as pltpu
from jax.sharding import PartitionSpec as P

VISCOSITY = 0.05
IMPLICIT = 0.05
ITERS = 4
MESH = pl.DeviceIdType.MESH

LANES = 128
SUB = 8
HALO = 8
PAD = 8


def lane_ids():
    return lax.broadcasted_iota(jnp.int32, (SUB, LANES), 1)


def roll(x, shift):
    return pltpu.roll(x, shift % LANES, axis=1)


def from_east(tiles, lane, by=1):
    rolled = [None if x is None else roll(x, -by) for x in tiles]
    out = []
    for n in range(len(tiles)):
        a, b = rolled[n], rolled[(n + 1) % len(tiles)]
        a = 0.0 if a is None else a
        b = 0.0 if b is None else b
        out.append(jnp.where(lane >= LANES - by, b, a))
    return out


def from_west(tiles, lane, by=1):
    rolled = [None if x is None else roll(x, by) for x in tiles]
    out = []
    for n in range(len(tiles)):
        a, b = rolled[n], rolled[n - 1]
        a = 0.0 if a is None else a
        b = 0.0 if b is None else b
        out.append(jnp.where(lane < by, b, a))
    return out


def scalars(nu):
    half = 0.5

    def times_b(s):
        return [s[1]] + [half * (s[n + 1] + s[n - 1]) for n in range(1, len(s) - 1)]

    def coef_b(c):
        out = [None] * (len(c) + 1)

        def put(n, x):
            out[n] = x if out[n] is None else out[n] + x

        for n, x in enumerate(c):
            if n == 0:
                put(1, x)
            else:
                put(n + 1, half * x)
                put(n - 1, half * x)
        zero = jnp.zeros_like(c[0])
        return [zero if x is None else x for x in out]

    def plus(a, b):
        n = max(len(a), len(b))
        return [
            a[m] + b[m] if m < len(a) and m < len(b) else (a[m] if m < len(a) else b[m])
            for m in range(n)
        ]

    one = jnp.ones_like(nu[0])
    s_z, s_d = list(nu), list(nu)
    c_z, c_d = [one], [one]
    c_p = []
    norm = nu[0]
    for it in range(ITERS):
        b = times_b(s_d)
        s_a = [s_d[n] - b[n] for n in range(len(b))]
        b = coef_b(c_d)
        c_a = plus(c_d, [-x for x in b])
        alpha = norm / (c_d[it] * s_a[it])
        c_p = plus(c_p, [alpha * x for x in c_d])
        c_z = plus(c_z, [-(alpha * x) for x in c_a])
        if it + 1 < ITERS:
            s_z = [s_z[n] - alpha * s_a[n] for n in range(len(s_a))]
            new = c_z[it + 1] * s_z[it + 1]
            beta = new / norm
            norm = new
            s_d = [s_z[n] + beta * s_d[n] for n in range(len(s_z))]
            c_d = plus(c_z, [beta * x for x in c_d])
    return c_p, c_z


def kernel(
    dims,
    th,
    fields,
    level_count,
    old_pressure,
    out_p,
    out_r,
    fb,
    lev,
    lp,
    pack,
    got1,
    got1d,
    fv,
    fr,
    ft,
    fold,
    got2y,
    got2x,
    got2d,
    c00,
    c0m,
    dm,
    dinv,
    q0,
    tk,
    mom,
    ar1,
    ar2,
    ores,
    load_sem,
    field_sem,
    send1,
    recv1,
    send2,
    recv2,
    sendr,
    recvr,
    sendc,
    recvc,
    out_sem,
):
    ny, nx, km, rows = dims
    ext = rows + 2 * HALO
    T = ext // SUB
    own = rows // SUB
    me_y, me_x = lax.axis_index("by"), lax.axis_index("bx")
    lane = lane_ids()
    sub = lax.broadcasted_iota(jnp.int32, (SUB, LANES), 0)
    zero = jnp.zeros((SUB, LANES), jnp.float32)

    loads = []
    for c in range(2):
        cols = pl.ds(c * LANES, LANES)
        loads.append(pltpu.make_async_copy(level_count.at[:, cols], lev.at[c], load_sem.at[c]))
        loads.append(
            pltpu.make_async_copy(
                old_pressure.at[:, cols], lp.at[1, c, pl.ds(PAD + HALO, rows)], load_sem.at[2 + c]
            )
        )
    for x in loads:
        x.start()

    def field_copy(k, c):
        return pltpu.make_async_copy(
            fields.at[:, k, :, pl.ds(c * LANES, LANES)],
            fb.at[:, k, c, pl.ds(PAD + HALO, rows)],
            field_sem.at[k, c],
        )

    for k in range(km):
        for c in range(2):
            field_copy(k, c).start()

    def peer(dy, dx):
        return (lax.rem(me_y + dy + ny, ny), lax.rem(me_x + dx + nx, nx))

    peers = [peer(dy, 0) for dy in range(1, ny)] + [peer(0, dx) for dx in range(1, nx)]
    peers += [peer(dy, dx) for dy in (1, -1) for dx in (1, -1)]
    barrier = pltpu.get_barrier_semaphore()
    for x in peers:
        pl.semaphore_signal(barrier, inc=1, device_id=x, device_id_type=MESH)

    def clear(k, carry):
        for f in range(3):
            for c in range(2):
                for r in (0, 8, rows + 16, rows + 24):
                    fb[f, k, c, pl.ds(r, SUB), :] = zero
        return carry

    lax.fori_loop(0, km, clear, 0)
    for n in range(2):
        for c in range(3):
            lp[n, c, pl.ds(0, SUB), :] = zero
            lp[n, c, pl.ds(ext + PAD, SUB), :] = zero

    def clear_sum(t, carry):
        for c in range(3):
            fv[t, c] = zero
            tk[0, t, c] = zero
        return carry

    lax.fori_loop(0, T, clear_sum, 0)

    for x in loads:
        x.wait()
    packed = [[zero] * 4, [zero] * 4]
    for r in range(own):
        at = pl.ds(PAD + HALO + r * SUB, SUB)
        group, pos = r % 8, r // 8
        mask = (lane >= 16 * group) & (lane < 16 * group + 16)
        for c in range(2):
            lp[0, c, at, :] = lev[c, pl.ds(r * SUB, SUB), :].astype(jnp.float32)
        east = jnp.where(lane >= 120, lp[0, 1, at, :], roll(lp[1, 1, at, :], -8))
        west = jnp.where(lane < 8, lp[0, 0, at, :], roll(lp[1, 0, at, :], 8))
        packed[0][pos] = jnp.where(mask, roll(east, 16 * group + 16), packed[0][pos])
        packed[1][pos] = jnp.where(mask, roll(west, 16 * group), packed[1][pos])
    for side in range(2):
        for pos in range(4):
            pack[side, pl.ds(pos * SUB, SUB), :] = packed[side][pos]
    pl.semaphore_wait(barrier, len(peers))

    def remote(src, dst, send, recv, n, target):
        return pltpu.make_async_remote_copy(
            src_ref=src,
            dst_ref=dst,
            send_sem=send.at[n],
            recv_sem=recv.at[n],
            device_id=target,
            device_id_type=MESH,
        )

    low, high = PAD + HALO, PAD + HALO + rows - SUB
    tiles01 = pl.ds(0, 2)
    first = [
        remote(lp.at[:, tiles01, pl.ds(high, SUB)], lp.at[:, tiles01, pl.ds(PAD, SUB)], send1, recv1, 0, peer(1, 0)),
        remote(lp.at[:, tiles01, pl.ds(low, SUB)], lp.at[:, tiles01, pl.ds(high + SUB, SUB)], send1, recv1, 1, peer(-1, 0)),
        remote(pack.at[0], got1.at[0], send1, recv1, 2, peer(0, 1)),
        remote(pack.at[1], got1.at[1], send1, recv1, 3, peer(0, -1)),
        remote(pack.at[0, pl.ds(24, SUB)], got1d.at[0], send1, recv1, 4, peer(1, 1)),
        remote(pack.at[1, pl.ds(24, SUB)], got1d.at[1], send1, recv1, 5, peer(1, -1)),
        remote(pack.at[0, pl.ds(0, SUB)], got1d.at[2], send1, recv1, 6, peer(-1, 1)),
        remote(pack.at[1, pl.ds(0, SUB)], got1d.at[3], send1, recv1, 7, peer(-1, -1)),
    ]
    for x in first:
        x.start()
    for x in first:
        x.wait_recv()

    def place(at, west_side, east_side, group):
        lev_w = roll(west_side, 112 - 16 * group)
        old_w = roll(west_side, 120 - 16 * group)
        lev_e = roll(east_side, -16 * group)
        old_e = roll(east_side, -16 * group - 8)
        lp[0, 2, at, :] = jnp.where(lane < 64, lev_e, lev_w)
        lp[1, 2, at, :] = jnp.where(lane < 64, old_e, old_w)

    for r in range(own):
        row = pl.ds((r // 8) * SUB, SUB)
        place(pl.ds(low + r * SUB, SUB), got1[0, row, :], got1[1, row, :], r % 8)
    place(pl.ds(PAD, SUB), got1d[0], got1d[1], 7)
    place(pl.ds(high + SUB, SUB), got1d[2], got1d[3], 0)

    def row_of(t):
        return pl.ds(t + PAD, SUB, stride=T)

    def level(k, carry):
        for c in range(2):
            field_copy(k, c).wait()
        weight = th[k] * (-0.5 * VISCOSITY)
        here = k.astype(jnp.float32)
        u, v, p, g, h = {}, {}, {}, {}, {}

        def load(f, t):
            return [fb[f, k, c, row_of(t), :] for c in range(2)]

        for step in range(-3, T + 3):
            v[step] = load(1, step)
            t = step - 1
            if -2 <= t:
                w = load(0, t) + [None]
                e, o = from_east(w, lane), from_west(w, lane)
                g[t] = [
                    (e[0] - o[0]) + (v[t + 1][0] - v[t - 1][0]),
                    (e[1] - o[1]) + (v[t + 1][1] - v[t - 1][1]),
                    e[2] - o[2],
                ]
                p[t] = load(2, t)
                v.pop(t - 1)
            t = step - 2
            if -1 <= t:
                e, o = from_east(g[t], lane), from_west(g[t], lane)
                h[t] = [
                    (e[c] + o[c]) + (g[t + 1][c] + g[t - 1][c]) - 4.0 * g[t][c] for c in range(3)
                ]
                g.pop(t - 1)
            t = step - 3
            if 0 <= t:
                e, o = from_east(h[t], lane), from_west(h[t], lane)
                ee, oo = from_east(p[t] + [None], lane, 2), from_west(p[t] + [None], lane, 2)
                for c in range(3):
                    bi = (e[c] + o[c]) + (h[t + 1][c] + h[t - 1][c]) - 4.0 * h[t][c]
                    pr = ee[c] + oo[c]
                    if c < 2:
                        pr = pr + (p[t + 2][c] + p[t - 2][c]) - 4.0 * p[t][c]
                    term = bi + (0.5 / VISCOSITY) * pr
                    wet = jnp.where(lp[0, c, row_of(t), :] > here, weight, 0.0)
                    fv[t, c] += wet * term
                h.pop(t - 1)
                p.pop(t - 2)
        return carry

    lax.fori_loop(0, km, level, 0)

    for t in range(T):
        for c in range(3):
            fr[c, pl.ds(t, SUB, stride=T), :] = fv[t, c]
    folded = [[zero] * 3, [zero] * 3]
    for r in range(T):
        at = pl.ds(r * SUB, SUB)
        group, pos = r % 12, r // 12
        mask = (lane >= 8 * group) & (lane < 8 * group + 8)
        east = roll(jnp.where(lane < 64, fr[2, at, :], fr[1, at, :]), 4 + 8 * group)
        west = roll(jnp.where(lane < 64, fr[0, at, :], fr[2, at, :]), 4 + 8 * group)
        folded[0][pos] = jnp.where(mask, east, folded[0][pos])
        folded[1][pos] = jnp.where(mask, west, folded[1][pos])
    for side in range(2):
        for pos in range(3):
            fold[side, pl.ds(pos * SUB, SUB), :] = folded[side][pos]
    second = [
        remote(fr.at[:, pl.ds(ext - 16, 16)], got2y.at[0], send2, recv2, 0, peer(1, 0)),
        remote(fr.at[:, pl.ds(0, 16)], got2y.at[1], send2, recv2, 1, peer(-1, 0)),
        remote(fold.at[0], got2x.at[0], send2, recv2, 2, peer(0, 1)),
        remote(fold.at[1], got2x.at[1], send2, recv2, 3, peer(0, -1)),
        remote(fold.at[0, pl.ds(16, SUB)], got2d.at[0], send2, recv2, 4, peer(1, 1)),
        remote(fold.at[1, pl.ds(16, SUB)], got2d.at[1], send2, recv2, 5, peer(1, -1)),
        remote(fold.at[0, pl.ds(0, SUB)], got2d.at[2], send2, recv2, 6, peer(-1, 1)),
        remote(fold.at[1, pl.ds(0, SUB)], got2d.at[3], send2, recv2, 7, peer(-1, -1)),
    ]
    for x in second:
        x.start()

    def depth_of(t):
        out = []
        for c in range(3):
            count = lp[0, c, row_of(t), :]
            total = jnp.where(count > 0.0, th[0], 0.0)
            for k in range(1, km):
                total = total + jnp.where(count > float(k), th[k], 0.0)
            out.append(total)
        return out

    def guess_of(t):
        return [jnp.where(lp[0, c, row_of(t), :] > 0.0, lp[1, c, row_of(t), :], 0.0) for c in range(3)]

    depth, mid, west, up, down = {-1: depth_of(-1)}, {}, {}, {}, {}
    for step in range(-1, T + 1):
        t = step
        if t < T:
            depth[t + 1] = depth_of(t + 1)
            low2 = [jnp.minimum(depth[t][c], depth[t + 1][c]) for c in range(3)]
            e = from_east(low2, lane)
            mid[t] = [0.5 * jnp.minimum(low2[c], e[c]) for c in range(3)]
            west[t] = from_west(mid[t], lane)
            depth.pop(t)
            for c in range(3):
                c00[t + 1, c] = mid[t][c]
                c0m[t + 1, c] = west[t][c]
        guess = guess_of(t)
        e, o = from_east(guess, lane), from_west(guess, lane)
        if t < T:
            down[t] = [mid[t][c] * e[c] + west[t][c] * o[c] for c in range(3)]
        if t >= 0:
            up[t] = [mid[t - 1][c] * e[c] + west[t - 1][c] * o[c] for c in range(3)]
        t = step - 1
        if t >= 0:
            guess = guess_of(t)
            for c in range(3):
                k_sum = (mid[t][c] + mid[t - 1][c]) + (west[t][c] + west[t - 1][c])
                diagonal = IMPLICIT + k_sum
                dinv[t, c] = 1.0 / diagonal
                q0[t, c] = (up[t + 1][c] + down[t - 1][c]) - k_sum * guess[c]
                if c < 2:
                    if t < HALO:
                        diagonal = jnp.where(sub == 0, 0.0, diagonal)
                    if t >= T - HALO:
                        diagonal = jnp.where(sub == SUB - 1, 0.0, diagonal)
                    dm[t, c] = diagonal
            mid.pop(t - 1), west.pop(t - 1), up.pop(t, None), down.pop(t - 1)

    for x in second:
        x.wait_recv()
    for r in range(T):
        at = pl.ds(r * SUB, SUB)
        group, pos = r % 12, pl.ds((r // 12) * SUB, SUB)
        shift = -(4 + 8 * group)
        east = roll(got2x[0, pos, :], shift)
        west_ = roll(got2x[1, pos, :], shift)
        total = [fr[c, at, :] for c in range(3)]
        if r < 2:
            total = [total[c] + got2y[0, c, at, :] for c in range(3)]
            east = east + roll(got2d[0], -(4 + 8 * (8 + r)))
            west_ = west_ + roll(got2d[1], -(4 + 8 * (8 + r)))
        if r >= T - 2:
            row = pl.ds((r - T + 2) * SUB, SUB)
            total = [total[c] + got2y[1, c, row, :] for c in range(3)]
            east = east + roll(got2d[2], -(4 + 8 * (r - T + 2)))
            west_ = west_ + roll(got2d[3], -(4 + 8 * (r - T + 2)))
        ft[0, at, :] = total[0] + jnp.where(lane < 4, east, 0.0)
        ft[1, at, :] = total[1] + jnp.where(lane >= 124, west_, 0.0)
        ft[2, at, :] = total[2] + jnp.where(lane < 4, west_, jnp.where(lane >= 124, east, 0.0))

    acc = [zero, zero]
    for t in range(T):
        for c in range(3):
            force = ft[c, pl.ds(t, SUB, stride=T), :]
            wet = lp[0, c, row_of(t), :] > 0.0
            z = (jnp.where(wet, force, 0.0) + q0[t, c]) * dinv[t, c]
            tk[1, t, c] = z
            if c < 2:
                acc[c] = acc[c] + (dm[t, c] * z) * z
    mom[0] = acc[0] + acc[1]

    def power(k, carry):
        factor = jnp.where(k == 0, 1.0, 2.0)

        def products(t):
            w = [tk[k + 1, t, c] for c in range(3)]
            e, o = from_east(w, lane), from_west(w, lane)
            dn = [c00[t + 1, c] * e[c] + c0m[t + 1, c] * o[c] for c in range(3)]
            up_ = [c00[t, c] * e[c] + c0m[t, c] * o[c] for c in range(3)]
            return w, dn, up_

        w_of, dn_of, up_of = {}, {}, {}
        w_of[T - 1], dn_of[T - 1], up_of[T - 1] = products(T - 1)
        dn_of[-1] = [pltpu.roll(x, 1, axis=0) for x in dn_of[T - 1]]
        w_of[0], dn_of[0], up_of[0] = products(0)
        up_of[T] = [pltpu.roll(x, SUB - 1, axis=0) for x in up_of[0]]
        odd, even = [zero, zero], [zero, zero]
        for t in range(T):
            if t + 1 < T - 1:
                w_of[t + 1], dn_of[t + 1], up_of[t + 1] = products(t + 1)
            for c in range(3):
                y = up_of[t + 1][c] + dn_of[t - 1][c]
                z = factor * (dinv[t, c] * y) - tk[k, t, c]
                tk[k + 2, t, c] = z
                if c < 2:
                    dz = dm[t, c] * z
                    odd[c] = odd[c] + dz * w_of[t][c]
                    even[c] = even[c] + dz * z
            dn_of.pop(t - 1), up_of.pop(t, None), w_of.pop(t)
        mom[2 * k + 1] = odd[0] + odd[1]
        mom[2 * k + 2] = even[0] + even[1]
        return carry

    lax.fori_loop(0, ITERS, power, 0)

    part = zero
    for n in range(2 * ITERS):
        part = jnp.where(sub == n, jnp.sum(mom[n], axis=0, keepdims=True), part)
    ar1[me_x] = part
    row_sum = [
        remote(ar1.at[me_x], ar1.at[me_x], sendr, recvr, o, peer(0, o)) for o in range(1, nx)
    ]
    for x in row_sum:
        x.start()
    for x in row_sum:
        x.wait_recv()
    part = sum_all(ar1, nx)
    ar2[me_y] = part
    col_sum = [
        remote(ar2.at[me_y], ar2.at[me_y], sendc, recvc, o, peer(o, 0)) for o in range(1, ny)
    ]
    for x in col_sum:
        x.start()
    for x in col_sum:
        x.wait_recv()
    whole = jnp.sum(sum_all(ar2, ny), axis=1, keepdims=True)
    raw = [jnp.broadcast_to(whole[n : n + 1, :], (SUB, LANES)) for n in range(2 * ITERS)]
    nu = [raw[0], raw[1]]
    for n in range(2, 2 * ITERS):
        nu.append(2.0 * raw[n] - nu[n % 2])
    c_p, c_z = scalars(nu)

    stores = []
    for n, out in ((0, out_p), (1, out_r)):
        for c in range(2):
            for t in range(T):
                if n == 0:
                    wet = lp[0, c, row_of(t), :] > 0.0
                    value = jnp.where(wet, lp[1, c, row_of(t), :], 0.0)
                    for m in range(ITERS):
                        value = value + c_p[m] * tk[m + 1, t, c]
                else:
                    value = c_z[0] * tk[1, t, c]
                    for m in range(1, ITERS + 1):
                        value = value + c_z[m] * tk[m + 1, t, c]
                    value = dm[t, c] * value
                ores[n, c, pl.ds(t, SUB, stride=T), :] = value
            stores.append(
                pltpu.make_async_copy(
                    ores.at[n, c, pl.ds(HALO, rows)],
                    out.at[:, pl.ds(c * LANES, LANES)],
                    out_sem.at[n, c],
                )
            )
            stores[-1].start()
    for x in first + second + row_sum + col_sum:
        x.wait_send()
    for x in stores:
        x.wait()


def sum_all(ref, count):
    parts = [ref[n] for n in range(count)]
    while len(parts) > 1:
        parts = [parts[n] + parts[n + 1] for n in range(0, len(parts), 2)]
    return parts[0]


def shards(ny, nx, fields, level_count, thickness, old_pressure):
    km, rows = fields.shape[1], fields.shape[2]
    ext = rows + 2 * HALO
    T = ext // SUB
    f32 = jnp.float32
    dma = pltpu.SemaphoreType.DMA
    vreg = (SUB, LANES)
    scratch = [
        pltpu.VMEM((3, km, 2, ext + 2 * PAD, LANES), f32),
        pltpu.VMEM((2, rows, LANES), jnp.int32),
        pltpu.VMEM((2, 3, ext + 2 * PAD, LANES), f32),
        pltpu.VMEM((2, 32, LANES), f32),
        pltpu.VMEM((2, 32, LANES), f32),
        pltpu.VMEM((4,) + vreg, f32),
        pltpu.VMEM((T, 3) + vreg, f32),
        pltpu.VMEM((3, ext, LANES), f32),
        pltpu.VMEM((3, ext, LANES), f32),
        pltpu.VMEM((2, 24, LANES), f32),
        pltpu.VMEM((2, 3, 16, LANES), f32),
        pltpu.VMEM((2, 24, LANES), f32),
        pltpu.VMEM((4,) + vreg, f32),
        pltpu.VMEM((T + 1, 3) + vreg, f32),
        pltpu.VMEM((T + 1, 3) + vreg, f32),
        pltpu.VMEM((T, 2) + vreg, f32),
        pltpu.VMEM((T, 3) + vreg, f32),
        pltpu.VMEM((T, 3) + vreg, f32),
        pltpu.VMEM((ITERS + 2, T, 3) + vreg, f32),
        pltpu.VMEM((2 * ITERS + 1,) + vreg, f32),
        pltpu.VMEM((nx,) + vreg, f32),
        pltpu.VMEM((ny,) + vreg, f32),
        pltpu.VMEM((2, 2, ext, LANES), f32),
        dma((4,)),
        dma((km, 2)),
        dma((8,)),
        dma((8,)),
        dma((8,)),
        dma((8,)),
        dma((nx,)),
        dma((nx,)),
        dma((ny,)),
        dma((ny,)),
        dma((2, 2)),
    ]
    shape = jax.ShapeDtypeStruct(old_pressure.shape, f32)
    anywhere = pl.BlockSpec(memory_space=pl.ANY)
    return pl.pallas_call(
        functools.partial(kernel, (ny, nx, km, rows)),
        out_shape=(shape, shape),
        in_specs=[pl.BlockSpec(memory_space=pltpu.SMEM), anywhere, anywhere, anywhere],
        out_specs=(anywhere, anywhere),
        scratch_shapes=scratch,
        compiler_params=pltpu.CompilerParams(
            collective_id=0, has_side_effects=True, vmem_limit_bytes=40 * 1024 * 1024
        ),
    )(thickness, fields, level_count, old_pressure)


def solution(mesh):
    ny, nx = mesh.shape["by"], mesh.shape["bx"]
    field = P("by", "bx")
    return jax.shard_map(
        functools.partial(shards, ny, nx),
        mesh=mesh,
        in_specs=(P(None, None, "by", "bx"), field, P(), field),
        out_specs=(field, field),
        check_vma=False,
    )
```

```python
import functools

import jax
import jax.numpy as jnp
from jax import lax
from jax.experimental import pallas as pl
from jax.experimental.pallas import tpu as pltpu
from jax.sharding import PartitionSpec as P

VISCOSITY = 0.05
IMPLICIT = 0.05
ITERS = 4
STEPS = 38
UNROLL = 19
REACH = 3
MESH = pl.DeviceIdType.MESH

LANES = 128
SUB = 8
HALO = 8
PAD = 8


def lane_ids():
    return lax.broadcasted_iota(jnp.int32, (SUB, LANES), 1)


def roll(x, shift):
    shift = shift % LANES if isinstance(shift, int) else lax.rem(shift + 2 * LANES, LANES)
    return pltpu.roll(x, shift, axis=1)


def steps(count, unroll, body, carry=()):
    def chunk(n, carry):
        for m in range(unroll):
            carry = body(n * unroll + m, carry)
        return carry

    return lax.fori_loop(0, count // unroll, chunk, carry)


def from_east(tiles, lane, by=1):
    rolled = [None if x is None else roll(x, -by) for x in tiles]
    out = []
    for n in range(len(tiles)):
        a, b = rolled[n], rolled[(n + 1) % len(tiles)]
        a = 0.0 if a is None else a
        b = 0.0 if b is None else b
        out.append(jnp.where(lane >= LANES - by, b, a))
    return out


def from_west(tiles, lane, by=1):
    rolled = [None if x is None else roll(x, by) for x in tiles]
    out = []
    for n in range(len(tiles)):
        a, b = rolled[n], rolled[n - 1]
        a = 0.0 if a is None else a
        b = 0.0 if b is None else b
        out.append(jnp.where(lane < by, b, a))
    return out


def scalars(nu):
    half = 0.5

    def times_b(s):
        return [s[1]] + [half * (s[n + 1] + s[n - 1]) for n in range(1, len(s) - 1)]

    def coef_b(c):
        out = [None] * (len(c) + 1)

        def put(n, x):
            out[n] = x if out[n] is None else out[n] + x

        for n, x in enumerate(c):
            if n == 0:
                put(1, x)
            else:
                put(n + 1, half * x)
                put(n - 1, half * x)
        zero = jnp.zeros_like(c[0])
        return [zero if x is None else x for x in out]

    def plus(a, b):
        n = max(len(a), len(b))
        return [
            a[m] + b[m] if m < len(a) and m < len(b) else (a[m] if m < len(a) else b[m])
            for m in range(n)
        ]

    one = jnp.ones_like(nu[0])
    s_z, s_d = list(nu), list(nu)
    c_z, c_d = [one], [one]
    c_p = []
    norm = nu[0]
    for it in range(ITERS):
        b = times_b(s_d)
        s_a = [s_d[n] - b[n] for n in range(len(b))]
        b = coef_b(c_d)
        c_a = plus(c_d, [-x for x in b])
        alpha = norm / (c_d[it] * s_a[it])
        c_p = plus(c_p, [alpha * x for x in c_d])
        c_z = plus(c_z, [-(alpha * x) for x in c_a])
        if it + 1 < ITERS:
            s_z = [s_z[n] - alpha * s_a[n] for n in range(len(s_a))]
            new = c_z[it + 1] * s_z[it + 1]
            beta = new / norm
            norm = new
            s_d = [s_z[n] + beta * s_d[n] for n in range(len(s_z))]
            c_d = plus(c_z, [beta * x for x in c_d])
    return c_p, c_z


def kernel(
    dims,
    th,
    fields,
    level_count,
    old_pressure,
    ores,
    fb,
    lev,
    lp,
    pack,
    got1,
    got1d,
    fv,
    lcs,
    fr,
    ft,
    fold,
    got2y,
    got2x,
    got2d,
    c00,
    c0m,
    dm,
    dinv,
    q0,
    tk,
    mom,
    ar1,
    ar2,
    load_sem,
    field_sem,
    send1,
    recv1,
    send2,
    recv2,
    sendr,
    recvr,
    sendc,
    recvc,
):
    ny, nx, km, rows = dims
    ext = rows + 2 * HALO
    T = ext // SUB
    before = STEPS - T
    me_y, me_x = lax.axis_index("by"), lax.axis_index("bx")
    lane = lane_ids()
    sub = lax.broadcasted_iota(jnp.int32, (SUB, LANES), 0)
    zero = jnp.zeros((SUB, LANES), jnp.float32)

    loads = []
    for c in range(2):
        cols = pl.ds(c * LANES, LANES)
        loads.append(pltpu.make_async_copy(level_count.at[:, cols], lev.at[c], load_sem.at[c]))
        loads.append(
            pltpu.make_async_copy(
                old_pressure.at[:, cols], lp.at[1, c, pl.ds(PAD + HALO, rows)], load_sem.at[2 + c]
            )
        )
    for x in loads:
        x.start()

    def field_copy(k, c):
        return pltpu.make_async_copy(
            fields.at[:, k, :, pl.ds(c * LANES, LANES)],
            fb.at[:, k, c, pl.ds(PAD + HALO, rows)],
            field_sem.at[k, c],
        )

    for k in range(km):
        for c in range(2):
            field_copy(k, c).start()

    def peer(dy, dx):
        return (lax.rem(me_y + dy + ny, ny), lax.rem(me_x + dx + nx, nx))

    peers = [peer(dy, 0) for dy in range(1, ny)] + [peer(0, dx) for dx in range(1, nx)]
    peers += [peer(dy, dx) for dy in (1, -1) for dx in (1, -1)]
    barrier = pltpu.get_barrier_semaphore()
    for x in peers:
        pl.semaphore_signal(barrier, inc=1, device_id=x, device_id_type=MESH)

    def clear(k, carry):
        for f in range(3):
            for c in range(2):
                for r in (0, 8, rows + 16, rows + 24):
                    fb[f, k, c, pl.ds(r, SUB), :] = zero
        return carry

    lax.fori_loop(0, km, clear, 0)
    for n in range(2):
        for c in range(3):
            lp[n, c, pl.ds(0, SUB), :] = zero
            lp[n, c, pl.ds(ext + PAD, SUB), :] = zero

    for c in range(3):
        for r in range(T, T + 2):
            fr[c, pl.ds(r * SUB, SUB), :] = zero

    def clear_sum(t, carry):
        for c in range(3):
            tk[0, t, c] = zero
        for m in range(2 * REACH + 1):
            for c in range(2):
                fv[m, t + before, c] = zero
        return carry

    steps(T, 2, clear_sum, 0)

    for x in loads:
        x.wait()

    def pack_group(group, carry):
        mask = (lane >= 16 * group) & (lane < 16 * group + 16)
        out = []
        for pos in range(4):
            row = pl.multiple_of((pos * 8 + group) * SUB, SUB)
            at = pl.ds(PAD + HALO + row, SUB)
            count = [lev[c, pl.ds(row, SUB), :].astype(jnp.float32) for c in range(2)]
            for c in range(2):
                lp[0, c, at, :] = count[c]
            east = jnp.where(lane >= 120, count[1], roll(lp[1, 1, at, :], -8))
            west = jnp.where(lane < 8, count[0], roll(lp[1, 0, at, :], 8))
            out.append(jnp.where(mask, roll(east, 16 * group + 16), carry[2 * pos]))
            out.append(jnp.where(mask, roll(west, 16 * group), carry[2 * pos + 1]))
        return tuple(out)

    packed = steps(8, 2, pack_group, (zero,) * 8)
    for side in range(2):
        for pos in range(4):
            pack[side, pl.ds(pos * SUB, SUB), :] = packed[2 * pos + side]
    pl.semaphore_wait(barrier, len(peers))

    def remote(src, dst, send, recv, n, target):
        return pltpu.make_async_remote_copy(
            src_ref=src,
            dst_ref=dst,
            send_sem=send.at[n],
            recv_sem=recv.at[n],
            device_id=target,
            device_id_type=MESH,
        )

    low, high = PAD + HALO, PAD + HALO + rows - SUB
    tiles01 = pl.ds(0, 2)
    first = [
        remote(lp.at[:, tiles01, pl.ds(high, SUB)], lp.at[:, tiles01, pl.ds(PAD, SUB)], send1, recv1, 0, peer(1, 0)),
        remote(lp.at[:, tiles01, pl.ds(low, SUB)], lp.at[:, tiles01, pl.ds(high + SUB, SUB)], send1, recv1, 1, peer(-1, 0)),
        remote(pack.at[0], got1.at[0], send1, recv1, 2, peer(0, 1)),
        remote(pack.at[1], got1.at[1], send1, recv1, 3, peer(0, -1)),
        remote(pack.at[0, pl.ds(24, SUB)], got1d.at[0], send1, recv1, 4, peer(1, 1)),
        remote(pack.at[1, pl.ds(24, SUB)], got1d.at[1], send1, recv1, 5, peer(1, -1)),
        remote(pack.at[0, pl.ds(0, SUB)], got1d.at[2], send1, recv1, 6, peer(-1, 1)),
        remote(pack.at[1, pl.ds(0, SUB)], got1d.at[3], send1, recv1, 7, peer(-1, -1)),
    ]
    for x in first:
        x.start()
    for x in first:
        x.wait_recv()

    def place(at, west_side, east_side, group):
        lev_w = roll(west_side, 112 - 16 * group)
        old_w = roll(west_side, 120 - 16 * group)
        lev_e = roll(east_side, -16 * group)
        old_e = roll(east_side, -16 * group - 8)
        lp[0, 2, at, :] = jnp.where(lane < 64, lev_e, lev_w)
        lp[1, 2, at, :] = jnp.where(lane < 64, old_e, old_w)

    def unpack_group(group, carry):
        for pos in range(4):
            row = pl.ds(pos * SUB, SUB)
            at = pl.ds(low + pl.multiple_of((pos * 8 + group) * SUB, SUB), SUB)
            place(at, got1[0, row, :], got1[1, row, :], group)
        return carry

    steps(8, 2, unpack_group, 0)
    place(pl.ds(PAD, SUB), got1d[0], got1d[1], 7)
    place(pl.ds(high + SUB, SUB), got1d[2], got1d[3], 0)

    def row_of(t):
        return pl.ds(t + PAD, SUB, stride=T)

    def shift_counts(group, carry):
        words = []
        for c in range(3):
            word = None
            for r in range(7):
                count = lp[0, c, row_of(group * 7 + r), :].astype(jnp.int32)
                word = count if r == 0 else word | (count << (4 * r))
            words.append(word)
        for m in range(-REACH, REACH + 1):
            moved = words
            if m > 0:
                moved = from_west(words, lane, m)
            elif m < 0:
                moved = from_east(words, lane, -m)
            for c in range(2):
                for r in range(7):
                    lcs[m + REACH, group * 7 + r + before, c] = (moved[c] >> (4 * r)) & 15
        return carry

    steps(-(-T // 7), 1, shift_counts, 0)

    def level(k, carry):
        for c in range(2):
            field_copy(k, c).wait()
        scale = th[k] * (-0.5 * VISCOSITY)
        scale_u = 2.0 * scale
        scale_p = (0.5 / VISCOSITY) * scale

        def load(f, t):
            return [fb[f, k, c, row_of(t), :] for c in range(2)]

        def row_step(n, carry):
            t = n - before
            u0, u1, a0, a1, v0, v1, e0, e1, p0, p1, p2, p3 = carry
            u2, p4 = load(0, t + 2), load(2, t + 2)
            north, south = load(1, t + 3), load(1, t + 1)
            out = [[] for _ in carry]
            for c in range(2):
                u2_ = u2[c] * scale_u
                p4_ = p4[c] * scale_p
                v2 = (north[c] - south[c]) * scale
                a2 = (u2_ + u0[c]) - 4.0 * u1[c]
                e2 = (v2 + v0[c]) - 4.0 * v1[c]
                b = v0[c] + p2[c]
                d = 4.0 * e1[c]
                odd = u0[c] + ((a2 + a0[c]) - 4.0 * a1[c])
                here = ((e2 + e0[c]) + (p4_ + p0[c])) - 4.0 * (e1[c] + p2[c]) + (v0[c] + v0[c])
                terms = [None, b - a1[c], d - odd, here, d + odd, b + a1[c], u0[c]]
                for m, term in enumerate(terms):
                    wet = lcs[m, n, c] > k
                    if m == 0:
                        fv[m, n, c] -= jnp.where(wet, u0[c], 0.0)
                    else:
                        fv[m, n, c] += jnp.where(wet, term, 0.0)
                row = (u1[c], u2_, a1[c], a2, v1[c], v2, e1[c], e2, p1[c], p2[c], p3[c], p4_)
                for x, y in zip(out, row):
                    x.append(y)
            return tuple(out)

        steps(STEPS, UNROLL, row_step, ([zero] * 2,) * 12)
        return carry

    lax.fori_loop(0, km, level, 0)

    def to_rows(t, carry):
        tiles = [[fv[m, t + before, c] for c in range(2)] + [None] for m in range(2 * REACH + 1)]
        total = [tiles[REACH][0], tiles[REACH][1], 0.0]
        for m in range(1, REACH + 1):
            scale = 1.0 if m == 2 else 0.5
            e = from_east(tiles[REACH + m], lane, m)
            o = from_west(tiles[REACH - m], lane, m)
            total = [total[c] + scale * (e[c] + o[c]) for c in range(3)]
        for c in range(3):
            fr[c, pl.ds(t, SUB, stride=T), :] = total[c]
        return carry

    steps(T, 2, to_rows, 0)

    def fold_group(group, carry):
        mask = (lane >= 8 * group) & (lane < 8 * group + 8)
        out = []
        for pos in range(3):
            at = pl.ds(pl.multiple_of((pos * 12 + group) * SUB, SUB), SUB)
            east = roll(jnp.where(lane < 64, fr[2, at, :], fr[1, at, :]), 4 + 8 * group)
            west = roll(jnp.where(lane < 64, fr[0, at, :], fr[2, at, :]), 4 + 8 * group)
            out.append(jnp.where(mask, east, carry[2 * pos]))
            out.append(jnp.where(mask, west, carry[2 * pos + 1]))
        return tuple(out)

    folded = steps(12, 2, fold_group, (zero,) * 6)
    for side in range(2):
        for pos in range(3):
            fold[side, pl.ds(pos * SUB, SUB), :] = folded[2 * pos + side]
    second = [
        remote(fr.at[:, pl.ds(ext - 16, 16)], got2y.at[0], send2, recv2, 0, peer(1, 0)),
        remote(fr.at[:, pl.ds(0, 16)], got2y.at[1], send2, recv2, 1, peer(-1, 0)),
        remote(fold.at[0], got2x.at[0], send2, recv2, 2, peer(0, 1)),
        remote(fold.at[1], got2x.at[1], send2, recv2, 3, peer(0, -1)),
        remote(fold.at[0, pl.ds(16, SUB)], got2d.at[0], send2, recv2, 4, peer(1, 1)),
        remote(fold.at[1, pl.ds(16, SUB)], got2d.at[1], send2, recv2, 5, peer(1, -1)),
        remote(fold.at[0, pl.ds(0, SUB)], got2d.at[2], send2, recv2, 6, peer(-1, 1)),
        remote(fold.at[1, pl.ds(0, SUB)], got2d.at[3], send2, recv2, 7, peer(-1, -1)),
    ]
    for x in second:
        x.start()

    def depth_of(t):
        out = []
        for c in range(3):
            count = lp[0, c, row_of(t), :]
            total = jnp.where(count > 0.0, th[0], 0.0)
            for k in range(1, km):
                total = total + jnp.where(count > float(k), th[k], 0.0)
            out.append(total)
        return out

    def guess_of(t):
        return [jnp.where(lp[0, c, row_of(t), :] > 0.0, lp[1, c, row_of(t), :], 0.0) for c in range(3)]

    def coefficient_step(n, carry):
        t = n - 1
        depth0, mid0, west0, down0, down1, k0, guess0 = carry
        depth1 = depth_of(t + 1)
        low2 = [jnp.minimum(depth0[c], depth1[c]) for c in range(3)]
        e = from_east(low2, lane)
        mid1 = [0.5 * jnp.minimum(low2[c], e[c]) for c in range(3)]
        west1 = from_west(mid1, lane)
        guess1 = guess_of(t)
        e, o = from_east(guess1, lane), from_west(guess1, lane)
        down2 = [mid1[c] * e[c] + west1[c] * o[c] for c in range(3)]
        k1 = [(mid1[c] + mid0[c]) + (west1[c] + west0[c]) for c in range(3)]
        outside = ((sub == 0) & (t - 1 < HALO)) | ((sub == SUB - 1) & (t - 1 >= T - HALO))
        for c in range(3):
            c00[n, c] = mid1[c]
            c0m[n, c] = west1[c]
            up = mid0[c] * e[c] + west0[c] * o[c]
            diagonal = IMPLICIT + k0[c]
            dinv[n, c] = 1.0 / diagonal
            q0[n, c] = (up + down0[c]) - k0[c] * guess0[c]
            if c < 2:
                dm[n, c] = jnp.where(outside, 0.0, diagonal)
        return depth1, mid1, west1, down1, down2, k1, guess1

    steps(T + 2, 4, coefficient_step, (depth_of(-1),) + ([zero] * 3,) * 6)

    for x in second:
        x.wait_recv()

    def gather_group(group, carry):
        for pos in range(3):
            at = pl.ds(pl.multiple_of((pos * 12 + group) * SUB, SUB), SUB)
            row = pl.ds(pos * SUB, SUB)
            east = roll(got2x[0, row, :], -(4 + 8 * group))
            west = roll(got2x[1, row, :], -(4 + 8 * group))
            ft[0, at, :] = fr[0, at, :] + jnp.where(lane < 4, east, 0.0)
            ft[1, at, :] = fr[1, at, :] + jnp.where(lane >= 124, west, 0.0)
            ft[2, at, :] = fr[2, at, :] + jnp.where(lane < 4, west, jnp.where(lane >= 124, east, 0.0))
        return carry

    steps(12, 2, gather_group, 0)
    for n in range(2):
        for side in range(2):
            row = pl.ds(n * SUB, SUB)
            at = pl.ds((T - 2 + n if side else n) * SUB, SUB)
            shift = -(4 + 8 * (n if side else 8 + n))
            east = roll(got2d[2 * side], shift)
            west = roll(got2d[2 * side + 1], shift)
            ft[0, at, :] += got2y[side, 0, row, :] + jnp.where(lane < 4, east, 0.0)
            ft[1, at, :] += got2y[side, 1, row, :] + jnp.where(lane >= 124, west, 0.0)
            ft[2, at, :] += got2y[side, 2, row, :] + jnp.where(
                lane < 4, west, jnp.where(lane >= 124, east, 0.0)
            )

    def residual_step(t, carry):
        out = []
        for c in range(3):
            force = ft[c, pl.ds(t, SUB, stride=T), :]
            wet = lp[0, c, row_of(t), :] > 0.0
            z = (jnp.where(wet, force, 0.0) + q0[t + 2, c]) * dinv[t + 2, c]
            tk[1, t, c] = z
            if c < 2:
                out.append(carry[c] + (dm[t + 2, c] * z) * z)
        return tuple(out)

    acc = steps(T, 2, residual_step, (zero, zero))
    mom[0] = acc[0] + acc[1]

    def power(k, carry):
        factor = jnp.where(k == 0, 1.0, 2.0)

        def products(t):
            w = [tk[k + 1, t, c] for c in range(3)]
            e, o = from_east(w, lane), from_west(w, lane)
            dn = [c00[t + 1, c] * e[c] + c0m[t + 1, c] * o[c] for c in range(3)]
            up_ = [c00[t, c] * e[c] + c0m[t, c] * o[c] for c in range(3)]
            return w, dn, up_

        w_of, dn_of, up_of = {}, {}, {}
        w_of[T - 1], dn_of[T - 1], up_of[T - 1] = products(T - 1)
        dn_of[-1] = [pltpu.roll(x, 1, axis=0) for x in dn_of[T - 1]]
        w_of[0], dn_of[0], up_of[0] = products(0)
        up_of[T] = [pltpu.roll(x, SUB - 1, axis=0) for x in up_of[0]]
        odd, even = [zero, zero], [zero, zero]
        for t in range(T):
            if t + 1 < T - 1:
                w_of[t + 1], dn_of[t + 1], up_of[t + 1] = products(t + 1)
            for c in range(3):
                y = up_of[t + 1][c] + dn_of[t - 1][c]
                z = factor * (dinv[t + 2, c] * y) - tk[k, t, c]
                tk[k + 2, t, c] = z
                if c < 2:
                    dz = dm[t + 2, c] * z
                    odd[c] = odd[c] + dz * w_of[t][c]
                    even[c] = even[c] + dz * z
            dn_of.pop(t - 1), up_of.pop(t, None), w_of.pop(t)
        mom[2 * k + 1] = odd[0] + odd[1]
        mom[2 * k + 2] = even[0] + even[1]
        return carry

    lax.fori_loop(0, ITERS, power, 0)

    part = zero
    for n in range(2 * ITERS):
        part = jnp.where(sub == n, jnp.sum(mom[n], axis=0, keepdims=True), part)
    ar1[me_x] = part
    row_sum = [
        remote(ar1.at[me_x], ar1.at[me_x], sendr, recvr, o, peer(0, o)) for o in range(1, nx)
    ]
    for x in row_sum:
        x.start()
    for x in row_sum:
        x.wait_recv()
    part = sum_all(ar1, nx)
    ar2[me_y] = part
    col_sum = [
        remote(ar2.at[me_y], ar2.at[me_y], sendc, recvc, o, peer(o, 0)) for o in range(1, ny)
    ]
    for x in col_sum:
        x.start()
    for x in col_sum:
        x.wait_recv()
    whole = jnp.sum(sum_all(ar2, ny), axis=1, keepdims=True)
    raw = [jnp.broadcast_to(whole[n : n + 1, :], (SUB, LANES)) for n in range(2 * ITERS)]
    nu = [raw[0], raw[1]]
    for n in range(2, 2 * ITERS):
        nu.append(2.0 * raw[n] - nu[n % 2])
    c_p, c_z = scalars(nu)

    def output_step(t, carry):
        for c in range(2):
            z = [tk[m + 1, t, c] for m in range(ITERS + 1)]
            wet = lp[0, c, row_of(t), :] > 0.0
            value = jnp.where(wet, lp[1, c, row_of(t), :], 0.0)
            for m in range(ITERS):
                value = value + c_p[m] * z[m]
            ores[0, c, pl.ds(t, SUB, stride=T), :] = value
            value = c_z[0] * z[0]
            for m in range(1, ITERS + 1):
                value = value + c_z[m] * z[m]
            ores[1, c, pl.ds(t, SUB, stride=T), :] = dm[t + 2, c] * value
        return carry

    steps(T, 2, output_step, 0)
    for x in first + second + row_sum + col_sum:
        x.wait_send()


def write_out(rows, ores, out_p, out_r, sem):
    stores = [
        pltpu.make_async_copy(
            ores.at[n, c, pl.ds(HALO, rows)], out.at[:, pl.ds(c * LANES, LANES)], sem.at[n, c]
        )
        for n, out in ((0, out_p), (1, out_r))
        for c in range(2)
    ]
    for x in stores:
        x.start()
    for x in stores:
        x.wait()


def sum_all(ref, count):
    parts = [ref[n] for n in range(count)]
    while len(parts) > 1:
        parts = [parts[n] + parts[n + 1] for n in range(0, len(parts), 2)]
    return parts[0]


def shards(ny, nx, fields, level_count, thickness, old_pressure):
    km, rows = fields.shape[1], fields.shape[2]
    ext = rows + 2 * HALO
    T = ext // SUB
    f32 = jnp.float32
    dma = pltpu.SemaphoreType.DMA
    vreg = (SUB, LANES)
    scratch = [
        pltpu.VMEM((3, km, 2, ext + 2 * PAD, LANES), f32),
        pltpu.VMEM((2, rows, LANES), jnp.int32),
        pltpu.VMEM((2, 3, ext + 2 * PAD, LANES), f32),
        pltpu.VMEM((2, 32, LANES), f32),
        pltpu.VMEM((2, 32, LANES), f32),
        pltpu.VMEM((4,) + vreg, f32),
        pltpu.VMEM((2 * REACH + 1, STEPS, 2) + vreg, f32),
        pltpu.VMEM((2 * REACH + 1, STEPS + 1, 2) + vreg, jnp.int32),
        pltpu.VMEM((3, ext + 2 * SUB, LANES), f32),
        pltpu.VMEM((3, ext + 2 * SUB, LANES), f32),
        pltpu.VMEM((2, 24, LANES), f32),
        pltpu.VMEM((2, 3, 16, LANES), f32),
        pltpu.VMEM((2, 24, LANES), f32),
        pltpu.VMEM((4,) + vreg, f32),
        pltpu.VMEM((T + 2, 3) + vreg, f32),
        pltpu.VMEM((T + 2, 3) + vreg, f32),
        pltpu.VMEM((T + 2, 2) + vreg, f32),
        pltpu.VMEM((T + 2, 3) + vreg, f32),
        pltpu.VMEM((T + 2, 3) + vreg, f32),
        pltpu.VMEM((ITERS + 2, T, 3) + vreg, f32),
        pltpu.VMEM((2 * ITERS + 1,) + vreg, f32),
        pltpu.VMEM((nx,) + vreg, f32),
        pltpu.VMEM((ny,) + vreg, f32),
        dma((4,)),
        dma((km, 2)),
        dma((8,)),
        dma((8,)),
        dma((8,)),
        dma((8,)),
        dma((nx,)),
        dma((nx,)),
        dma((ny,)),
        dma((ny,)),
    ]
    hbm = pl.BlockSpec(memory_space=pltpu.HBM)
    vmem = pl.BlockSpec(memory_space=pltpu.VMEM)
    result = pl.pallas_call(
        functools.partial(kernel, (ny, nx, km, rows)),
        out_shape=pltpu.VMEM((2, 2, ext, LANES), f32),
        in_specs=[pl.BlockSpec(memory_space=pltpu.SMEM), hbm, hbm, hbm],
        out_specs=vmem,
        scratch_shapes=scratch,
        compiler_params=pltpu.CompilerParams(
            collective_id=0, has_side_effects=True, vmem_limit_bytes=58 * 1024 * 1024
        ),
    )(thickness, fields, level_count, old_pressure)
    shape = jax.ShapeDtypeStruct(old_pressure.shape, f32)
    return pl.pallas_call(
        functools.partial(write_out, rows),
        out_shape=(shape, shape),
        in_specs=[pl.BlockSpec(memory_space=pl.ANY)],
        out_specs=(hbm, hbm),
        scratch_shapes=[dma((2, 2))],
        compiler_params=pltpu.CompilerParams(vmem_limit_bytes=4 * 1024 * 1024),
    )(result)


def solution(mesh):
    ny, nx = mesh.shape["by"], mesh.shape["bx"]
    field = P("by", "bx")
    return jax.shard_map(
        functools.partial(shards, ny, nx),
        mesh=mesh,
        in_specs=(P(None, None, "by", "bx"), field, P(), field),
        out_specs=(field, field),
        check_vma=False,
    )
```

```python
import functools

import jax
import jax.numpy as jnp
from jax import lax
from jax.experimental import pallas as pl
from jax.experimental.pallas import tpu as pltpu
from jax.sharding import PartitionSpec as P

VISCOSITY = 0.05
IMPLICIT = 0.05
ITERS = 4
STEPS = 38
UNROLL = 19
UNROLL_SUM = 2
REACH = 3
MESH = pl.DeviceIdType.MESH

LANES = 128
SUB = 8
HALO = 8
PAD = 8


def lane_ids():
    return lax.broadcasted_iota(jnp.int32, (SUB, LANES), 1)


def roll(x, shift):
    shift = shift % LANES if isinstance(shift, int) else lax.rem(shift + 2 * LANES, LANES)
    return pltpu.roll(x, shift, axis=1)


def steps(count, unroll, body, carry=()):
    def chunk(n, carry):
        for m in range(unroll):
            carry = body(n * unroll + m, carry)
        return carry

    return lax.fori_loop(0, count // unroll, chunk, carry)


def from_east(tiles, lane, by=1):
    rolled = [None if x is None else roll(x, -by) for x in tiles]
    out = []
    for n in range(len(tiles)):
        a, b = rolled[n], rolled[(n + 1) % len(tiles)]
        a = 0.0 if a is None else a
        b = 0.0 if b is None else b
        out.append(jnp.where(lane >= LANES - by, b, a))
    return out


def from_west(tiles, lane, by=1):
    rolled = [None if x is None else roll(x, by) for x in tiles]
    out = []
    for n in range(len(tiles)):
        a, b = rolled[n], rolled[n - 1]
        a = 0.0 if a is None else a
        b = 0.0 if b is None else b
        out.append(jnp.where(lane < by, b, a))
    return out


def scalars(nu):
    half = 0.5

    def times_b(s):
        return [s[1]] + [half * (s[n + 1] + s[n - 1]) for n in range(1, len(s) - 1)]

    def coef_b(c):
        out = [None] * (len(c) + 1)

        def put(n, x):
            out[n] = x if out[n] is None else out[n] + x

        for n, x in enumerate(c):
            if n == 0:
                put(1, x)
            else:
                put(n + 1, half * x)
                put(n - 1, half * x)
        zero = jnp.zeros_like(c[0])
        return [zero if x is None else x for x in out]

    def plus(a, b):
        n = max(len(a), len(b))
        return [
            a[m] + b[m] if m < len(a) and m < len(b) else (a[m] if m < len(a) else b[m])
            for m in range(n)
        ]

    one = jnp.ones_like(nu[0])
    s_z, s_d = list(nu), list(nu)
    c_z, c_d = [one], [one]
    c_p = []
    norm = nu[0]
    for it in range(ITERS):
        b = times_b(s_d)
        s_a = [s_d[n] - b[n] for n in range(len(b))]
        b = coef_b(c_d)
        c_a = plus(c_d, [-x for x in b])
        alpha = norm / (c_d[it] * s_a[it])
        c_p = plus(c_p, [alpha * x for x in c_d])
        c_z = plus(c_z, [-(alpha * x) for x in c_a])
        if it + 1 < ITERS:
            s_z = [s_z[n] - alpha * s_a[n] for n in range(len(s_a))]
            new = c_z[it + 1] * s_z[it + 1]
            beta = new / norm
            norm = new
            s_d = [s_z[n] + beta * s_d[n] for n in range(len(s_z))]
            c_d = plus(c_z, [beta * x for x in c_d])
    return c_p, c_z


def kernel(
    dims,
    th,
    fields,
    level_count,
    old_pressure,
    ores,
    fb,
    lev,
    lp,
    pack,
    got1,
    got1d,
    terms,
    lcs,
    fr,
    ft,
    fold,
    got2y,
    got2x,
    got2d,
    c00,
    c0m,
    dm,
    dinv,
    q0,
    tk,
    mom,
    ar1,
    ar2,
    load_sem,
    field_sem,
    send1,
    recv1,
    send2,
    recv2,
    sendr,
    recvr,
    sendc,
    recvc,
):
    ny, nx, km, rows = dims
    ext = rows + 2 * HALO
    T = ext // SUB
    before = STEPS - T
    me_y, me_x = lax.axis_index("by"), lax.axis_index("bx")
    lane = lane_ids()
    sub = lax.broadcasted_iota(jnp.int32, (SUB, LANES), 0)
    zero = jnp.zeros((SUB, LANES), jnp.float32)

    loads = []
    for c in range(2):
        cols = pl.ds(c * LANES, LANES)
        loads.append(pltpu.make_async_copy(level_count.at[:, cols], lev.at[c], load_sem.at[c]))
        loads.append(
            pltpu.make_async_copy(
                old_pressure.at[:, cols], lp.at[1, c, pl.ds(PAD + HALO, rows)], load_sem.at[2 + c]
            )
        )
    for x in loads:
        x.start()

    def field_copy(k, c):
        return pltpu.make_async_copy(
            fields.at[:, k, :, pl.ds(c * LANES, LANES)],
            fb.at[:, k, c, pl.ds(PAD + HALO, rows)],
            field_sem.at[k, c],
        )

    for k in range(km):
        for c in range(2):
            field_copy(k, c).start()

    def peer(dy, dx):
        return (lax.rem(me_y + dy + ny, ny), lax.rem(me_x + dx + nx, nx))

    peers = [peer(dy, 0) for dy in range(1, ny)] + [peer(0, dx) for dx in range(1, nx)]
    peers += [peer(dy, dx) for dy in (1, -1) for dx in (1, -1)]
    barrier = pltpu.get_barrier_semaphore()
    for x in peers:
        pl.semaphore_signal(barrier, inc=1, device_id=x, device_id_type=MESH)

    def clear(k, carry):
        for f in range(3):
            for c in range(2):
                for r in (0, 8, rows + 16, rows + 24):
                    fb[f, k, c, pl.ds(r, SUB), :] = zero
        return carry

    lax.fori_loop(0, km, clear, 0)
    for n in range(2):
        for c in range(3):
            lp[n, c, pl.ds(0, SUB), :] = zero
            lp[n, c, pl.ds(ext + PAD, SUB), :] = zero

    for c in range(3):
        for r in range(T, T + 2):
            fr[c, pl.ds(r * SUB, SUB), :] = zero

    def clear_sum(t, carry):
        for c in range(3):
            tk[0, t, c] = zero
        return carry

    steps(T, 2, clear_sum, 0)

    for x in loads:
        x.wait()

    def pack_group(group, carry):
        mask = (lane >= 16 * group) & (lane < 16 * group + 16)
        out = []
        for pos in range(4):
            row = pl.multiple_of((pos * 8 + group) * SUB, SUB)
            at = pl.ds(PAD + HALO + row, SUB)
            count = [lev[c, pl.ds(row, SUB), :].astype(jnp.float32) for c in range(2)]
            for c in range(2):
                lp[0, c, at, :] = count[c]
            east = jnp.where(lane >= 120, count[1], roll(lp[1, 1, at, :], -8))
            west = jnp.where(lane < 8, count[0], roll(lp[1, 0, at, :], 8))
            out.append(jnp.where(mask, roll(east, 16 * group + 16), carry[2 * pos]))
            out.append(jnp.where(mask, roll(west, 16 * group), carry[2 * pos + 1]))
        return tuple(out)

    packed = steps(8, 2, pack_group, (zero,) * 8)
    for side in range(2):
        for pos in range(4):
            pack[side, pl.ds(pos * SUB, SUB), :] = packed[2 * pos + side]
    pl.semaphore_wait(barrier, len(peers))

    def remote(src, dst, send, recv, n, target):
        return pltpu.make_async_remote_copy(
            src_ref=src,
            dst_ref=dst,
            send_sem=send.at[n],
            recv_sem=recv.at[n],
            device_id=target,
            device_id_type=MESH,
        )

    low, high = PAD + HALO, PAD + HALO + rows - SUB
    tiles01 = pl.ds(0, 2)
    first = [
        remote(lp.at[:, tiles01, pl.ds(high, SUB)], lp.at[:, tiles01, pl.ds(PAD, SUB)], send1, recv1, 0, peer(1, 0)),
        remote(lp.at[:, tiles01, pl.ds(low, SUB)], lp.at[:, tiles01, pl.ds(high + SUB, SUB)], send1, recv1, 1, peer(-1, 0)),
        remote(pack.at[0], got1.at[0], send1, recv1, 2, peer(0, 1)),
        remote(pack.at[1], got1.at[1], send1, recv1, 3, peer(0, -1)),
        remote(pack.at[0, pl.ds(24, SUB)], got1d.at[0], send1, recv1, 4, peer(1, 1)),
        remote(pack.at[1, pl.ds(24, SUB)], got1d.at[1], send1, recv1, 5, peer(1, -1)),
        remote(pack.at[0, pl.ds(0, SUB)], got1d.at[2], send1, recv1, 6, peer(-1, 1)),
        remote(pack.at[1, pl.ds(0, SUB)], got1d.at[3], send1, recv1, 7, peer(-1, -1)),
    ]
    for x in first:
        x.start()
    def row_of(t):
        return pl.ds(t + PAD, SUB, stride=T)

    def level(k, carry):
        for c in range(2):
            field_copy(k, c).wait()
        scale = th[k] * (-0.5 * VISCOSITY)
        scale_u = 2.0 * scale
        scale_p = (0.5 / VISCOSITY) * scale

        def load(f, t):
            return [fb[f, k, c, row_of(t), :] for c in range(2)]

        def row_step(n, carry):
            t = n - before
            u0, u1, a0, a1, v0, v1, e0, e1, p0, p1, p2, p3 = carry
            u2, p4 = load(0, t + 2), load(2, t + 2)
            north, south = load(1, t + 3), load(1, t + 1)
            out = [[] for _ in carry]
            for c in range(2):
                u2_ = u2[c] * scale_u
                p4_ = p4[c] * scale_p
                v2 = (north[c] - south[c]) * scale
                a2 = (u2_ + u0[c]) - 4.0 * u1[c]
                e2 = (v2 + v0[c]) - 4.0 * v1[c]
                b = v0[c] + p2[c]
                d = 4.0 * e1[c]
                odd = u0[c] + ((a2 + a0[c]) - 4.0 * a1[c])
                here = ((e2 + e0[c]) + (p4_ + p0[c])) - 4.0 * (e1[c] + p2[c]) + (v0[c] + v0[c])
                for m, term in enumerate([u0[c], b - a1[c], d - odd, here, d + odd, b + a1[c]]):
                    terms[k, n, m, c] = term
                row = (u1[c], u2_, a1[c], a2, v1[c], v2, e1[c], e2, p1[c], p2[c], p3[c], p4_)
                for x, y in zip(out, row):
                    x.append(y)
            return tuple(out)

        steps(STEPS, UNROLL, row_step, ([zero] * 2,) * 12)
        return carry

    lax.fori_loop(0, km, level, 0)

    for x in first:
        x.wait_recv()

    def place(at, west_side, east_side, group):
        lev_w = roll(west_side, 112 - 16 * group)
        old_w = roll(west_side, 120 - 16 * group)
        lev_e = roll(east_side, -16 * group)
        old_e = roll(east_side, -16 * group - 8)
        lp[0, 2, at, :] = jnp.where(lane < 64, lev_e, lev_w)
        lp[1, 2, at, :] = jnp.where(lane < 64, old_e, old_w)

    def unpack_group(group, carry):
        for pos in range(4):
            row = pl.ds(pos * SUB, SUB)
            at = pl.ds(low + pl.multiple_of((pos * 8 + group) * SUB, SUB), SUB)
            place(at, got1[0, row, :], got1[1, row, :], group)
        return carry

    steps(8, 2, unpack_group, 0)
    place(pl.ds(PAD, SUB), got1d[0], got1d[1], 7)
    place(pl.ds(high + SUB, SUB), got1d[2], got1d[3], 0)

    def shift_counts(group, carry):
        words = []
        for c in range(3):
            word = None
            for r in range(7):
                count = lp[0, c, row_of(group * 7 + r), :].astype(jnp.int32)
                word = count if r == 0 else word | (count << (4 * r))
            words.append(word)
        for m in range(-REACH, REACH + 1):
            moved = words
            if m > 0:
                moved = from_west(words, lane, m)
            elif m < 0:
                moved = from_east(words, lane, -m)
            for c in range(2):
                for r in range(7):
                    lcs[group * 7 + r, m + REACH, c] = (moved[c] >> (4 * r)) & 15
        return carry

    steps(-(-T // 7), 1, shift_counts, 0)

    def to_rows(t, carry):
        tiles = []
        for m in range(2 * REACH + 1):
            sums = []
            for c in range(2):
                count = lcs[t, m, c]
                total = None
                for k in range(km):
                    term = jnp.where(count > k, terms[k, t + before, m % (2 * REACH), c], 0.0)
                    total = term if k == 0 else total + term
                sums.append(total)
            tiles.append(sums + [None])
        total = [tiles[REACH][0], tiles[REACH][1], 0.0]
        for m in range(1, REACH + 1):
            e = from_east(tiles[REACH + m], lane, m)
            o = from_west(tiles[REACH - m], lane, m)
            for c in range(3):
                both = e[c] - o[c] if m == 3 else e[c] + o[c]
                total[c] = total[c] + (both if m == 2 else 0.5 * both)
        for c in range(3):
            fr[c, pl.ds(t, SUB, stride=T), :] = total[c]
        return carry

    steps(T, UNROLL_SUM, to_rows, 0)

    def fold_group(group, carry):
        mask = (lane >= 8 * group) & (lane < 8 * group + 8)
        out = []
        for pos in range(3):
            at = pl.ds(pl.multiple_of((pos * 12 + group) * SUB, SUB), SUB)
            east = roll(jnp.where(lane < 64, fr[2, at, :], fr[1, at, :]), 4 + 8 * group)
            west = roll(jnp.where(lane < 64, fr[0, at, :], fr[2, at, :]), 4 + 8 * group)
            out.append(jnp.where(mask, east, carry[2 * pos]))
            out.append(jnp.where(mask, west, carry[2 * pos + 1]))
        return tuple(out)

    folded = steps(12, 2, fold_group, (zero,) * 6)
    for side in range(2):
        for pos in range(3):
            fold[side, pl.ds(pos * SUB, SUB), :] = folded[2 * pos + side]
    second = [
        remote(fr.at[:, pl.ds(ext - 16, 16)], got2y.at[0], send2, recv2, 0, peer(1, 0)),
        remote(fr.at[:, pl.ds(0, 16)], got2y.at[1], send2, recv2, 1, peer(-1, 0)),
        remote(fold.at[0], got2x.at[0], send2, recv2, 2, peer(0, 1)),
        remote(fold.at[1], got2x.at[1], send2, recv2, 3, peer(0, -1)),
        remote(fold.at[0, pl.ds(16, SUB)], got2d.at[0], send2, recv2, 4, peer(1, 1)),
        remote(fold.at[1, pl.ds(16, SUB)], got2d.at[1], send2, recv2, 5, peer(1, -1)),
        remote(fold.at[0, pl.ds(0, SUB)], got2d.at[2], send2, recv2, 6, peer(-1, 1)),
        remote(fold.at[1, pl.ds(0, SUB)], got2d.at[3], send2, recv2, 7, peer(-1, -1)),
    ]
    for x in second:
        x.start()

    def depth_of(t):
        out = []
        for c in range(3):
            count = lp[0, c, row_of(t), :]
            total = jnp.where(count > 0.0, th[0], 0.0)
            for k in range(1, km):
                total = total + jnp.where(count > float(k), th[k], 0.0)
            out.append(total)
        return out

    def guess_of(t):
        return [jnp.where(lp[0, c, row_of(t), :] > 0.0, lp[1, c, row_of(t), :], 0.0) for c in range(3)]

    def coefficient_step(n, carry):
        t = n - 1
        depth0, mid0, west0, down0, down1, k0, guess0 = carry
        depth1 = depth_of(t + 1)
        low2 = [jnp.minimum(depth0[c], depth1[c]) for c in range(3)]
        e = from_east(low2, lane)
        mid1 = [0.5 * jnp.minimum(low2[c], e[c]) for c in range(3)]
        west1 = from_west(mid1, lane)
        guess1 = guess_of(t)
        e, o = from_east(guess1, lane), from_west(guess1, lane)
        down2 = [mid1[c] * e[c] + west1[c] * o[c] for c in range(3)]
        k1 = [(mid1[c] + mid0[c]) + (west1[c] + west0[c]) for c in range(3)]
        outside = ((sub == 0) & (t - 1 < HALO)) | ((sub == SUB - 1) & (t - 1 >= T - HALO))
        for c in range(3):
            c00[n, c] = mid1[c]
            c0m[n, c] = west1[c]
            up = mid0[c] * e[c] + west0[c] * o[c]
            diagonal = IMPLICIT + k0[c]
            dinv[n, c] = 1.0 / diagonal
            q0[n, c] = (up + down0[c]) - k0[c] * guess0[c]
            if c < 2:
                dm[n, c] = jnp.where(outside, 0.0, diagonal)
        return depth1, mid1, west1, down1, down2, k1, guess1

    steps(T + 2, 4, coefficient_step, (depth_of(-1),) + ([zero] * 3,) * 6)

    for x in second:
        x.wait_recv()

    def gather_group(group, carry):
        for pos in range(3):
            at = pl.ds(pl.multiple_of((pos * 12 + group) * SUB, SUB), SUB)
            row = pl.ds(pos * SUB, SUB)
            east = roll(got2x[0, row, :], -(4 + 8 * group))
            west = roll(got2x[1, row, :], -(4 + 8 * group))
            ft[0, at, :] = fr[0, at, :] + jnp.where(lane < 4, east, 0.0)
            ft[1, at, :] = fr[1, at, :] + jnp.where(lane >= 124, west, 0.0)
            ft[2, at, :] = fr[2, at, :] + jnp.where(lane < 4, west, jnp.where(lane >= 124, east, 0.0))
        return carry

    steps(12, 2, gather_group, 0)
    for n in range(2):
        for side in range(2):
            row = pl.ds(n * SUB, SUB)
            at = pl.ds((T - 2 + n if side else n) * SUB, SUB)
            shift = -(4 + 8 * (n if side else 8 + n))
            east = roll(got2d[2 * side], shift)
            west = roll(got2d[2 * side + 1], shift)
            ft[0, at, :] += got2y[side, 0, row, :] + jnp.where(lane < 4, east, 0.0)
            ft[1, at, :] += got2y[side, 1, row, :] + jnp.where(lane >= 124, west, 0.0)
            ft[2, at, :] += got2y[side, 2, row, :] + jnp.where(
                lane < 4, west, jnp.where(lane >= 124, east, 0.0)
            )

    def residual_step(t, carry):
        out = []
        for c in range(3):
            force = ft[c, pl.ds(t, SUB, stride=T), :]
            wet = lp[0, c, row_of(t), :] > 0.0
            z = (jnp.where(wet, force, 0.0) + q0[t + 2, c]) * dinv[t + 2, c]
            tk[1, t, c] = z
            if c < 2:
                out.append(carry[c] + (dm[t + 2, c] * z) * z)
        return tuple(out)

    acc = steps(T, 2, residual_step, (zero, zero))
    mom[0] = acc[0] + acc[1]

    def power(k, carry):
        factor = jnp.where(k == 0, 1.0, 2.0)

        def products(t):
            w = [tk[k + 1, t, c] for c in range(3)]
            e, o = from_east(w, lane), from_west(w, lane)
            dn = [c00[t + 1, c] * e[c] + c0m[t + 1, c] * o[c] for c in range(3)]
            up_ = [c00[t, c] * e[c] + c0m[t, c] * o[c] for c in range(3)]
            return w, dn, up_

        w_of, dn_of, up_of = {}, {}, {}
        w_of[T - 1], dn_of[T - 1], up_of[T - 1] = products(T - 1)
        dn_of[-1] = [pltpu.roll(x, 1, axis=0) for x in dn_of[T - 1]]
        w_of[0], dn_of[0], up_of[0] = products(0)
        up_of[T] = [pltpu.roll(x, SUB - 1, axis=0) for x in up_of[0]]
        odd, even = [zero, zero], [zero, zero]
        for t in range(T):
            if t + 1 < T - 1:
                w_of[t + 1], dn_of[t + 1], up_of[t + 1] = products(t + 1)
            for c in range(3):
                y = up_of[t + 1][c] + dn_of[t - 1][c]
                z = factor * (dinv[t + 2, c] * y) - tk[k, t, c]
                tk[k + 2, t, c] = z
                if c < 2:
                    dz = dm[t + 2, c] * z
                    odd[c] = odd[c] + dz * w_of[t][c]
                    even[c] = even[c] + dz * z
            dn_of.pop(t - 1), up_of.pop(t, None), w_of.pop(t)
        mom[2 * k + 1] = odd[0] + odd[1]
        mom[2 * k + 2] = even[0] + even[1]
        return carry

    lax.fori_loop(0, ITERS, power, 0)

    part = zero
    for n in range(2 * ITERS):
        part = jnp.where(sub == n, jnp.sum(mom[n], axis=0, keepdims=True), part)
    ar1[me_y] = part
    col_sum = [
        remote(ar1.at[me_y], ar1.at[me_y], sendr, recvr, o, peer(o, 0)) for o in range(1, ny)
    ]
    for x in col_sum:
        x.start()
    for x in col_sum:
        x.wait_recv()
    part = sum_all(ar1, ny)
    ar2[me_x] = part
    row_sum = [
        remote(ar2.at[me_x], ar2.at[me_x], sendc, recvc, o, peer(0, o)) for o in range(1, nx)
    ]
    for x in row_sum:
        x.start()
    for x in row_sum:
        x.wait_recv()
    whole = jnp.sum(sum_all(ar2, nx), axis=1, keepdims=True)
    raw = [jnp.broadcast_to(whole[n : n + 1, :], (SUB, LANES)) for n in range(2 * ITERS)]
    nu = [raw[0], raw[1]]
    for n in range(2, 2 * ITERS):
        nu.append(2.0 * raw[n] - nu[n % 2])
    c_p, c_z = scalars(nu)

    def output_step(t, carry):
        for c in range(2):
            z = [tk[m + 1, t, c] for m in range(ITERS + 1)]
            wet = lp[0, c, row_of(t), :] > 0.0
            value = jnp.where(wet, lp[1, c, row_of(t), :], 0.0)
            for m in range(ITERS):
                value = value + c_p[m] * z[m]
            ores[0, c, pl.ds(t, SUB, stride=T), :] = value
            value = c_z[0] * z[0]
            for m in range(1, ITERS + 1):
                value = value + c_z[m] * z[m]
            ores[1, c, pl.ds(t, SUB, stride=T), :] = dm[t + 2, c] * value
        return carry

    steps(T, 2, output_step, 0)
    for x in first + second + row_sum + col_sum:
        x.wait_send()


def write_out(rows, ores, out_p, out_r, sem):
    stores = [
        pltpu.make_async_copy(
            ores.at[n, c, pl.ds(HALO, rows)], out.at[:, pl.ds(c * LANES, LANES)], sem.at[n, c]
        )
        for n, out in ((0, out_p), (1, out_r))
        for c in range(2)
    ]
    for x in stores:
        x.start()
    for x in stores:
        x.wait()


def sum_all(ref, count):
    parts = [ref[n] for n in range(count)]
    while len(parts) > 1:
        parts = [parts[n] + parts[n + 1] for n in range(0, len(parts), 2)]
    return parts[0]


def shards(ny, nx, fields, level_count, thickness, old_pressure):
    km, rows = fields.shape[1], fields.shape[2]
    ext = rows + 2 * HALO
    T = ext // SUB
    f32 = jnp.float32
    dma = pltpu.SemaphoreType.DMA
    vreg = (SUB, LANES)
    scratch = [
        pltpu.VMEM((3, km, 2, ext + 2 * PAD, LANES), f32),
        pltpu.VMEM((2, rows, LANES), jnp.int32),
        pltpu.VMEM((2, 3, ext + 2 * PAD, LANES), f32),
        pltpu.VMEM((2, 32, LANES), f32),
        pltpu.VMEM((2, 32, LANES), f32),
        pltpu.VMEM((4,) + vreg, f32),
        pltpu.VMEM((km, STEPS, 2 * REACH, 2) + vreg, f32),
        pltpu.VMEM((T + 1, 2 * REACH + 1, 2) + vreg, jnp.int32),
        pltpu.VMEM((3, ext + 2 * SUB, LANES), f32),
        pltpu.VMEM((3, ext + 2 * SUB, LANES), f32),
        pltpu.VMEM((2, 24, LANES), f32),
        pltpu.VMEM((2, 3, 16, LANES), f32),
        pltpu.VMEM((2, 24, LANES), f32),
        pltpu.VMEM((4,) + vreg, f32),
        pltpu.VMEM((T + 2, 3) + vreg, f32),
        pltpu.VMEM((T + 2, 3) + vreg, f32),
        pltpu.VMEM((T + 2, 2) + vreg, f32),
        pltpu.VMEM((T + 2, 3) + vreg, f32),
        pltpu.VMEM((T + 2, 3) + vreg, f32),
        pltpu.VMEM((ITERS + 2, T, 3) + vreg, f32),
        pltpu.VMEM((2 * ITERS + 1,) + vreg, f32),
        pltpu.VMEM((ny,) + vreg, f32),
        pltpu.VMEM((nx,) + vreg, f32),
        dma((4,)),
        dma((km, 2)),
        dma((8,)),
        dma((8,)),
        dma((8,)),
        dma((8,)),
        dma((ny,)),
        dma((ny,)),
        dma((nx,)),
        dma((nx,)),
    ]
    hbm = pl.BlockSpec(memory_space=pltpu.HBM)
    vmem = pl.BlockSpec(memory_space=pltpu.VMEM)
    result = pl.pallas_call(
        functools.partial(kernel, (ny, nx, km, rows)),
        out_shape=pltpu.VMEM((2, 2, ext, LANES), f32),
        in_specs=[pl.BlockSpec(memory_space=pltpu.SMEM), hbm, hbm, hbm],
        out_specs=vmem,
        scratch_shapes=scratch,
        compiler_params=pltpu.CompilerParams(
            collective_id=0, has_side_effects=True, vmem_limit_bytes=58 * 1024 * 1024
        ),
    )(thickness, fields, level_count, old_pressure)
    shape = jax.ShapeDtypeStruct(old_pressure.shape, f32)
    return pl.pallas_call(
        functools.partial(write_out, rows),
        out_shape=(shape, shape),
        in_specs=[pl.BlockSpec(memory_space=pl.ANY)],
        out_specs=(hbm, hbm),
        scratch_shapes=[dma((2, 2))],
        compiler_params=pltpu.CompilerParams(vmem_limit_bytes=4 * 1024 * 1024),
    )(result)


def solution(mesh):
    ny, nx = mesh.shape["by"], mesh.shape["bx"]
    field = P("by", "bx")
    return jax.shard_map(
        functools.partial(shards, ny, nx),
        mesh=mesh,
        in_specs=(P(None, None, "by", "bx"), field, P(), field),
        out_specs=(field, field),
        check_vma=False,
    )
```

```python
import functools

import jax
import jax.numpy as jnp
from jax import lax
from jax.experimental import pallas as pl
from jax.experimental.pallas import tpu as pltpu
from jax.sharding import PartitionSpec as P

VISCOSITY = 0.05
IMPLICIT = 0.05
ITERS = 4
STEPS = 38
UNROLL = 19
UNROLL_SUM = 17
REACH = 3
MESH = pl.DeviceIdType.MESH

LANES = 128
SUB = 8
HALO = 8
PAD = 8


def lane_ids():
    return lax.broadcasted_iota(jnp.int32, (SUB, LANES), 1)


def roll(x, shift):
    shift = shift % LANES if isinstance(shift, int) else lax.rem(shift + 2 * LANES, LANES)
    return pltpu.roll(x, shift, axis=1)


def steps(count, unroll, body, carry=()):
    def chunk(n, carry):
        for m in range(unroll):
            carry = body(n * unroll + m, carry)
        return carry

    return lax.fori_loop(0, count // unroll, chunk, carry)


def from_east(tiles, lane, by=1):
    rolled = [None if x is None else roll(x, -by) for x in tiles]
    out = []
    for n in range(len(tiles)):
        a, b = rolled[n], rolled[(n + 1) % len(tiles)]
        a = 0.0 if a is None else a
        b = 0.0 if b is None else b
        out.append(jnp.where(lane >= LANES - by, b, a))
    return out


def from_west(tiles, lane, by=1):
    rolled = [None if x is None else roll(x, by) for x in tiles]
    out = []
    for n in range(len(tiles)):
        a, b = rolled[n], rolled[n - 1]
        a = 0.0 if a is None else a
        b = 0.0 if b is None else b
        out.append(jnp.where(lane < by, b, a))
    return out


def scalars(nu):
    half = 0.5

    def times_b(s):
        return [s[1]] + [half * (s[n + 1] + s[n - 1]) for n in range(1, len(s) - 1)]

    def coef_b(c):
        out = [None] * (len(c) + 1)

        def put(n, x):
            out[n] = x if out[n] is None else out[n] + x

        for n, x in enumerate(c):
            if n == 0:
                put(1, x)
            else:
                put(n + 1, half * x)
                put(n - 1, half * x)
        zero = jnp.zeros_like(c[0])
        return [zero if x is None else x for x in out]

    def plus(a, b):
        n = max(len(a), len(b))
        return [
            a[m] + b[m] if m < len(a) and m < len(b) else (a[m] if m < len(a) else b[m])
            for m in range(n)
        ]

    one = jnp.ones_like(nu[0])
    s_z, s_d = list(nu), list(nu)
    c_z, c_d = [one], [one]
    c_p = []
    norm = nu[0]
    for it in range(ITERS):
        b = times_b(s_d)
        s_a = [s_d[n] - b[n] for n in range(len(b))]
        b = coef_b(c_d)
        c_a = plus(c_d, [-x for x in b])
        alpha = norm / (c_d[it] * s_a[it])
        c_p = plus(c_p, [alpha * x for x in c_d])
        c_z = plus(c_z, [-(alpha * x) for x in c_a])
        if it + 1 < ITERS:
            s_z = [s_z[n] - alpha * s_a[n] for n in range(len(s_a))]
            new = c_z[it + 1] * s_z[it + 1]
            beta = new / norm
            norm = new
            s_d = [s_z[n] + beta * s_d[n] for n in range(len(s_z))]
            c_d = plus(c_z, [beta * x for x in c_d])
    return c_p, c_z


def kernel(
    dims,
    th,
    fields,
    level_count,
    old_pressure,
    ores,
    fb,
    lev,
    lp,
    pack,
    got1,
    got1d,
    terms,
    lcs,
    fr,
    ft,
    fold,
    got2y,
    got2x,
    got2d,
    c00,
    c0m,
    dm,
    dinv,
    q0,
    tk,
    mom,
    ar1,
    ar2,
    load_sem,
    field_sem,
    send1,
    recv1,
    send2,
    recv2,
    sendr,
    recvr,
    sendc,
    recvc,
):
    ny, nx, km, rows = dims
    ext = rows + 2 * HALO
    T = ext // SUB
    before = STEPS - T
    me_y, me_x = lax.axis_index("by"), lax.axis_index("bx")
    lane = lane_ids()
    sub = lax.broadcasted_iota(jnp.int32, (SUB, LANES), 0)
    zero = jnp.zeros((SUB, LANES), jnp.float32)

    def peer(dy, dx):
        return (lax.rem(me_y + dy + ny, ny), lax.rem(me_x + dx + nx, nx))

    peers = [peer(dy, 0) for dy in range(1, ny)] + [peer(0, dx) for dx in range(1, nx)]
    peers += [peer(dy, dx) for dy in (1, -1) for dx in (1, -1)]
    barrier = pltpu.get_barrier_semaphore()
    for x in peers:
        pl.semaphore_signal(barrier, inc=1, device_id=x, device_id_type=MESH)

    loads = []
    for c in range(2):
        cols = pl.ds(c * LANES, LANES)
        loads.append(pltpu.make_async_copy(level_count.at[:, cols], lev.at[c], load_sem.at[c]))
        loads.append(
            pltpu.make_async_copy(
                old_pressure.at[:, cols], lp.at[1, c, pl.ds(PAD + HALO, rows)], load_sem.at[2 + c]
            )
        )
    for x in loads:
        x.start()

    def field_copy(k, c):
        return pltpu.make_async_copy(
            fields.at[:, k, :, pl.ds(c * LANES, LANES)],
            fb.at[:, k, c, pl.ds(PAD + HALO, rows)],
            field_sem.at[k, c],
        )

    for k in range(km):
        for c in range(2):
            field_copy(k, c).start()

    def clear(k, carry):
        for f in range(3):
            for c in range(2):
                for r in (0, 8, rows + 16, rows + 24):
                    fb[f, k, c, pl.ds(r, SUB), :] = zero
        return carry

    lax.fori_loop(0, km, clear, 0)
    for n in range(2):
        for c in range(3):
            lp[n, c, pl.ds(0, SUB), :] = zero
            lp[n, c, pl.ds(ext + PAD, SUB), :] = zero

    for c in range(3):
        for r in range(T, T + 2):
            fr[c, pl.ds(r * SUB, SUB), :] = zero

    def clear_sum(t, carry):
        for c in range(3):
            tk[0, t, c] = zero
        return carry

    steps(T, 2, clear_sum, 0)

    def clear_terms(n, carry):
        for m in range(2 * REACH):
            for c in range(2):
                terms[0, n, m, c] = zero
        return carry

    steps(STEPS, 2, clear_terms, 0)

    for x in loads:
        x.wait()

    def pack_group(group, carry):
        mask = (lane >= 16 * group) & (lane < 16 * group + 16)
        out = []
        for pos in range(4):
            row = pl.multiple_of((pos * 8 + group) * SUB, SUB)
            at = pl.ds(PAD + HALO + row, SUB)
            count = [lev[c, pl.ds(row, SUB), :].astype(jnp.float32) for c in range(2)]
            for c in range(2):
                lp[0, c, at, :] = count[c]
            east = jnp.where(lane >= 120, count[1], roll(lp[1, 1, at, :], -8))
            west = jnp.where(lane < 8, count[0], roll(lp[1, 0, at, :], 8))
            out.append(jnp.where(mask, roll(east, 16 * group + 16), carry[2 * pos]))
            out.append(jnp.where(mask, roll(west, 16 * group), carry[2 * pos + 1]))
        return tuple(out)

    packed = steps(8, 2, pack_group, (zero,) * 8)
    for side in range(2):
        for pos in range(4):
            pack[side, pl.ds(pos * SUB, SUB), :] = packed[2 * pos + side]
    pl.semaphore_wait(barrier, len(peers))

    def remote(src, dst, send, recv, n, target):
        return pltpu.make_async_remote_copy(
            src_ref=src,
            dst_ref=dst,
            send_sem=send.at[n],
            recv_sem=recv.at[n],
            device_id=target,
            device_id_type=MESH,
        )

    low, high = PAD + HALO, PAD + HALO + rows - SUB
    tiles01 = pl.ds(0, 2)
    first = [
        remote(lp.at[:, tiles01, pl.ds(high, SUB)], lp.at[:, tiles01, pl.ds(PAD, SUB)], send1, recv1, 0, peer(1, 0)),
        remote(lp.at[:, tiles01, pl.ds(low, SUB)], lp.at[:, tiles01, pl.ds(high + SUB, SUB)], send1, recv1, 1, peer(-1, 0)),
        remote(pack.at[0], got1.at[0], send1, recv1, 2, peer(0, 1)),
        remote(pack.at[1], got1.at[1], send1, recv1, 3, peer(0, -1)),
        remote(pack.at[0, pl.ds(24, SUB)], got1d.at[0], send1, recv1, 4, peer(1, 1)),
        remote(pack.at[1, pl.ds(24, SUB)], got1d.at[1], send1, recv1, 5, peer(1, -1)),
        remote(pack.at[0, pl.ds(0, SUB)], got1d.at[2], send1, recv1, 6, peer(-1, 1)),
        remote(pack.at[1, pl.ds(0, SUB)], got1d.at[3], send1, recv1, 7, peer(-1, -1)),
    ]
    for x in first:
        x.start()
    def row_of(t):
        return pl.ds(t + PAD, SUB, stride=T)

    def level(k, carry):
        for c in range(2):
            field_copy(k, c).wait()
        scale = th[k] * (-0.5 * VISCOSITY)
        scale_u = 2.0 * scale
        scale_p = (0.5 / VISCOSITY) * scale

        def load(f, t):
            return [fb[f, k, c, row_of(t), :] for c in range(2)]

        def row_step(n, carry):
            t = n - before
            u0, u1, a0, a1, v0, v1, e0, e1, p0, p1, p2, p3 = carry
            u2, p4 = load(0, t + 2), load(2, t + 2)
            north, south = load(1, t + 3), load(1, t + 1)
            out = [[] for _ in carry]
            for c in range(2):
                u2_ = u2[c] * scale_u
                p4_ = p4[c] * scale_p
                v2 = (north[c] - south[c]) * scale
                a2 = (u2_ + u0[c]) - 4.0 * u1[c]
                e2 = (v2 + v0[c]) - 4.0 * v1[c]
                b = v0[c] + p2[c]
                d = 4.0 * e1[c]
                odd = u0[c] + ((a2 + a0[c]) - 4.0 * a1[c])
                here = ((e2 + e0[c]) + (p4_ + p0[c])) - 4.0 * (e1[c] + p2[c]) + (v0[c] + v0[c])
                for m, term in enumerate([u0[c], b - a1[c], d - odd, here, d + odd, b + a1[c]]):
                    terms[k + 1, n, m, c] = terms[k, n, m, c] + term
                row = (u1[c], u2_, a1[c], a2, v1[c], v2, e1[c], e2, p1[c], p2[c], p3[c], p4_)
                for x, y in zip(out, row):
                    x.append(y)
            return tuple(out)

        steps(STEPS, UNROLL, row_step, ([zero] * 2,) * 12)
        return carry

    lax.fori_loop(0, km, level, 0)

    for x in first:
        x.wait_recv()

    def unpack(n, shift_west, shift_east):
        def place(at, west_side, east_side, group):
            west = roll(west_side, shift_west - 16 * group)
            east = roll(east_side, shift_east - 16 * group)
            lp[n, 2, at, :] = jnp.where(lane < 64, east, west)

        def unpack_group(group, carry):
            for pos in range(4):
                row = pl.ds(pos * SUB, SUB)
                at = pl.ds(low + pl.multiple_of((pos * 8 + group) * SUB, SUB), SUB)
                place(at, got1[0, row, :], got1[1, row, :], group)
            return carry

        steps(8, 4, unpack_group, 0)
        place(pl.ds(PAD, SUB), got1d[0], got1d[1], 7)
        place(pl.ds(high + SUB, SUB), got1d[2], got1d[3], 0)

    unpack(0, 112, 0)

    def shift_counts(group, carry):
        words = []
        for c in range(3):
            word = None
            for r in range(7):
                count = lp[0, c, row_of(group * 7 + r), :].astype(jnp.int32)
                word = count if r == 0 else word | (count << (4 * r))
            words.append(word)
        for m in range(-REACH, REACH + 1):
            moved = words
            if m > 0:
                moved = from_west(words, lane, m)
            elif m < 0:
                moved = from_east(words, lane, -m)
            for c in range(2):
                for r in range(7):
                    lcs[group * 7 + r, m + REACH, c] = (moved[c] >> (4 * r)) & 15
        return carry

    steps(-(-T // 7), 5, shift_counts, 0)

    def to_rows(t, carry):
        tiles = []
        for m in range(2 * REACH + 1):
            sums = []
            for c in range(2):
                count = lcs[t, m, c]
                total = 0.0
                for k in range(km):
                    total = jnp.where(count > k, terms[k + 1, t + before, m % (2 * REACH), c], total)
                sums.append(total)
            tiles.append(sums + [None])
        total = [tiles[REACH][0], tiles[REACH][1], 0.0]
        for m in range(1, REACH + 1):
            e = from_east(tiles[REACH + m], lane, m)
            o = from_west(tiles[REACH - m], lane, m)
            for c in range(3):
                both = e[c] - o[c] if m == 3 else e[c] + o[c]
                total[c] = total[c] + (both if m == 2 else 0.5 * both)
        for c in range(3):
            fr[c, pl.ds(t, SUB, stride=T), :] = total[c]
        return carry

    steps(T, UNROLL_SUM, to_rows, 0)

    def fold_group(group, carry):
        mask = (lane >= 8 * group) & (lane < 8 * group + 8)
        out = []
        for pos in range(3):
            at = pl.ds(pl.multiple_of((pos * 12 + group) * SUB, SUB), SUB)
            east = roll(jnp.where(lane < 64, fr[2, at, :], fr[1, at, :]), 4 + 8 * group)
            west = roll(jnp.where(lane < 64, fr[0, at, :], fr[2, at, :]), 4 + 8 * group)
            out.append(jnp.where(mask, east, carry[2 * pos]))
            out.append(jnp.where(mask, west, carry[2 * pos + 1]))
        return tuple(out)

    folded = steps(12, 6, fold_group, (zero,) * 6)
    for side in range(2):
        for pos in range(3):
            fold[side, pl.ds(pos * SUB, SUB), :] = folded[2 * pos + side]
    second = [
        remote(fr.at[:, pl.ds(ext - 16, 16)], got2y.at[0], send2, recv2, 0, peer(1, 0)),
        remote(fr.at[:, pl.ds(0, 16)], got2y.at[1], send2, recv2, 1, peer(-1, 0)),
        remote(fold.at[0], got2x.at[0], send2, recv2, 2, peer(0, 1)),
        remote(fold.at[1], got2x.at[1], send2, recv2, 3, peer(0, -1)),
        remote(fold.at[0, pl.ds(16, SUB)], got2d.at[0], send2, recv2, 4, peer(1, 1)),
        remote(fold.at[1, pl.ds(16, SUB)], got2d.at[1], send2, recv2, 5, peer(1, -1)),
        remote(fold.at[0, pl.ds(0, SUB)], got2d.at[2], send2, recv2, 6, peer(-1, 1)),
        remote(fold.at[1, pl.ds(0, SUB)], got2d.at[3], send2, recv2, 7, peer(-1, -1)),
    ]
    for x in second:
        x.start()
    unpack(1, 120, -8)
    for x in first:
        x.wait_send()

    def depth_of(t):
        out = []
        for c in range(3):
            count = lp[0, c, row_of(t), :]
            total = jnp.where(count > 0.0, th[0], 0.0)
            for k in range(1, km):
                total = total + jnp.where(count > float(k), th[k], 0.0)
            out.append(total)
        return out

    def guess_of(t):
        return [jnp.where(lp[0, c, row_of(t), :] > 0.0, lp[1, c, row_of(t), :], 0.0) for c in range(3)]

    def coefficient_step(n, carry):
        t = n - 1
        depth0, mid0, west0, down0, down1, k0, guess0 = carry
        depth1 = depth_of(t + 1)
        low2 = [jnp.minimum(depth0[c], depth1[c]) for c in range(3)]
        e = from_east(low2, lane)
        mid1 = [0.5 * jnp.minimum(low2[c], e[c]) for c in range(3)]
        west1 = from_west(mid1, lane)
        guess1 = guess_of(t)
        e, o = from_east(guess1, lane), from_west(guess1, lane)
        down2 = [mid1[c] * e[c] + west1[c] * o[c] for c in range(3)]
        k1 = [(mid1[c] + mid0[c]) + (west1[c] + west0[c]) for c in range(3)]
        outside = ((sub == 0) & (t - 1 < HALO)) | ((sub == SUB - 1) & (t - 1 >= T - HALO))
        for c in range(3):
            c00[n, c] = mid1[c]
            c0m[n, c] = west1[c]
            up = mid0[c] * e[c] + west0[c] * o[c]
            diagonal = IMPLICIT + k0[c]
            dinv[n, c] = 1.0 / diagonal
            q0[n, c] = (up + down0[c]) - k0[c] * guess0[c]
            if c < 2:
                dm[n, c] = jnp.where(outside, 0.0, diagonal)
        return depth1, mid1, west1, down1, down2, k1, guess1

    steps(T + 2, 4, coefficient_step, (depth_of(-1),) + ([zero] * 3,) * 6)

    for x in second:
        x.wait_recv()

    def gather_group(group, carry):
        for pos in range(3):
            at = pl.ds(pl.multiple_of((pos * 12 + group) * SUB, SUB), SUB)
            row = pl.ds(pos * SUB, SUB)
            east = roll(got2x[0, row, :], -(4 + 8 * group))
            west = roll(got2x[1, row, :], -(4 + 8 * group))
            ft[0, at, :] = fr[0, at, :] + jnp.where(lane < 4, east, 0.0)
            ft[1, at, :] = fr[1, at, :] + jnp.where(lane >= 124, west, 0.0)
            ft[2, at, :] = fr[2, at, :] + jnp.where(lane < 4, west, jnp.where(lane >= 124, east, 0.0))
        return carry

    steps(12, 6, gather_group, 0)
    for n in range(2):
        for side in range(2):
            row = pl.ds(n * SUB, SUB)
            at = pl.ds((T - 2 + n if side else n) * SUB, SUB)
            shift = -(4 + 8 * (n if side else 8 + n))
            east = roll(got2d[2 * side], shift)
            west = roll(got2d[2 * side + 1], shift)
            ft[0, at, :] += got2y[side, 0, row, :] + jnp.where(lane < 4, east, 0.0)
            ft[1, at, :] += got2y[side, 1, row, :] + jnp.where(lane >= 124, west, 0.0)
            ft[2, at, :] += got2y[side, 2, row, :] + jnp.where(
                lane < 4, west, jnp.where(lane >= 124, east, 0.0)
            )

    def residual_step(t, carry):
        out = []
        for c in range(3):
            force = ft[c, pl.ds(t, SUB, stride=T), :]
            wet = lp[0, c, row_of(t), :] > 0.0
            z = (jnp.where(wet, force, 0.0) + q0[t + 2, c]) * dinv[t + 2, c]
            tk[1, t, c] = z
            if c < 2:
                out.append(carry[c] + (dm[t + 2, c] * z) * z)
        return tuple(out)

    acc = steps(T, 17, residual_step, (zero, zero))
    mom[0] = acc[0] + acc[1]

    def power(k, carry):
        factor = jnp.where(k == 0, 1.0, 2.0)

        def products(t):
            w = [tk[k + 1, t, c] for c in range(3)]
            e, o = from_east(w, lane), from_west(w, lane)
            dn = [c00[t + 1, c] * e[c] + c0m[t + 1, c] * o[c] for c in range(3)]
            up_ = [c00[t, c] * e[c] + c0m[t, c] * o[c] for c in range(3)]
            return w, dn, up_

        w_of, dn_of, up_of = {}, {}, {}
        w_of[T - 1], dn_of[T - 1], up_of[T - 1] = products(T - 1)
        dn_of[-1] = [pltpu.roll(x, 1, axis=0) for x in dn_of[T - 1]]
        w_of[0], dn_of[0], up_of[0] = products(0)
        up_of[T] = [pltpu.roll(x, SUB - 1, axis=0) for x in up_of[0]]
        odd, even = [zero, zero], [zero, zero]
        for t in range(T):
            if t + 1 < T - 1:
                w_of[t + 1], dn_of[t + 1], up_of[t + 1] = products(t + 1)
            for c in range(3):
                y = up_of[t + 1][c] + dn_of[t - 1][c]
                z = factor * (dinv[t + 2, c] * y) - tk[k, t, c]
                tk[k + 2, t, c] = z
                if c < 2:
                    dz = dm[t + 2, c] * z
                    odd[c] = odd[c] + dz * w_of[t][c]
                    even[c] = even[c] + dz * z
            dn_of.pop(t - 1), up_of.pop(t, None), w_of.pop(t)
        mom[2 * k + 1] = odd[0] + odd[1]
        mom[2 * k + 2] = even[0] + even[1]
        return carry

    lax.fori_loop(0, ITERS, power, 0)

    part = zero
    for n in range(2 * ITERS):
        part = jnp.where(sub == n, jnp.sum(mom[n], axis=0, keepdims=True), part)
    ar1[me_y] = part
    col_sum = [
        remote(ar1.at[me_y], ar1.at[me_y], sendr, recvr, o, peer(o, 0)) for o in range(1, ny)
    ]
    for x in col_sum:
        x.start()
    for x in second:
        x.wait_send()
    for x in col_sum:
        x.wait_recv()
    part = sum_all(ar1, ny)
    ar2[me_x] = part
    row_sum = [
        remote(ar2.at[me_x], ar2.at[me_x], sendc, recvc, o, peer(0, o)) for o in range(1, nx)
    ]
    for x in row_sum:
        x.start()
    for x in col_sum:
        x.wait_send()
    for x in row_sum:
        x.wait_recv()
    whole = jnp.sum(sum_all(ar2, nx), axis=1, keepdims=True)
    raw = [jnp.broadcast_to(whole[n : n + 1, :], (SUB, LANES)) for n in range(2 * ITERS)]
    nu = [raw[0], raw[1]]
    for n in range(2, 2 * ITERS):
        nu.append(2.0 * raw[n] - nu[n % 2])
    c_p, c_z = scalars(nu)

    def output_step(t, carry):
        for c in range(2):
            z = [tk[m + 1, t, c] for m in range(ITERS + 1)]
            wet = lp[0, c, row_of(t), :] > 0.0
            value = jnp.where(wet, lp[1, c, row_of(t), :], 0.0)
            for m in range(ITERS):
                value = value + c_p[m] * z[m]
            ores[0, c, pl.ds(t, SUB, stride=T), :] = value
            value = c_z[0] * z[0]
            for m in range(1, ITERS + 1):
                value = value + c_z[m] * z[m]
            ores[1, c, pl.ds(t, SUB, stride=T), :] = dm[t + 2, c] * value
        return carry

    steps(T, 17, output_step, 0)
    for x in row_sum:
        x.wait_send()


def write_out(rows, ores, out_p, out_r, sem):
    stores = [
        pltpu.make_async_copy(
            ores.at[n, c, pl.ds(HALO, rows)], out.at[:, pl.ds(c * LANES, LANES)], sem.at[n, c]
        )
        for n, out in ((0, out_p), (1, out_r))
        for c in range(2)
    ]
    for x in stores:
        x.start()
    for x in stores:
        x.wait()


def sum_all(ref, count):
    parts = [ref[n] for n in range(count)]
    while len(parts) > 1:
        parts = [parts[n] + parts[n + 1] for n in range(0, len(parts), 2)]
    return parts[0]


def shards(ny, nx, fields, level_count, thickness, old_pressure):
    km, rows = fields.shape[1], fields.shape[2]
    ext = rows + 2 * HALO
    T = ext // SUB
    f32 = jnp.float32
    dma = pltpu.SemaphoreType.DMA
    vreg = (SUB, LANES)
    scratch = [
        pltpu.VMEM((3, km, 2, ext + 2 * PAD, LANES), f32),
        pltpu.VMEM((2, rows, LANES), jnp.int32),
        pltpu.VMEM((2, 3, ext + 2 * PAD, LANES), f32),
        pltpu.VMEM((2, 32, LANES), f32),
        pltpu.VMEM((2, 32, LANES), f32),
        pltpu.VMEM((4,) + vreg, f32),
        pltpu.VMEM((km + 1, STEPS, 2 * REACH, 2) + vreg, f32),
        pltpu.VMEM((T + 1, 2 * REACH + 1, 2) + vreg, jnp.int32),
        pltpu.VMEM((3, ext + 2 * SUB, LANES), f32),
        pltpu.VMEM((3, ext + 2 * SUB, LANES), f32),
        pltpu.VMEM((2, 24, LANES), f32),
        pltpu.VMEM((2, 3, 16, LANES), f32),
        pltpu.VMEM((2, 24, LANES), f32),
        pltpu.VMEM((4,) + vreg, f32),
        pltpu.VMEM((T + 2, 3) + vreg, f32),
        pltpu.VMEM((T + 2, 3) + vreg, f32),
        pltpu.VMEM((T + 2, 2) + vreg, f32),
        pltpu.VMEM((T + 2, 3) + vreg, f32),
        pltpu.VMEM((T + 2, 3) + vreg, f32),
        pltpu.VMEM((ITERS + 2, T, 3) + vreg, f32),
        pltpu.VMEM((2 * ITERS + 1,) + vreg, f32),
        pltpu.VMEM((ny,) + vreg, f32),
        pltpu.VMEM((nx,) + vreg, f32),
        dma((4,)),
        dma((km, 2)),
        dma((8,)),
        dma((8,)),
        dma((8,)),
        dma((8,)),
        dma((ny,)),
        dma((ny,)),
        dma((nx,)),
        dma((nx,)),
    ]
    hbm = pl.BlockSpec(memory_space=pltpu.HBM)
    vmem = pl.BlockSpec(memory_space=pltpu.VMEM)
    result = pl.pallas_call(
        functools.partial(kernel, (ny, nx, km, rows)),
        out_shape=pltpu.VMEM((2, 2, ext, LANES), f32),
        in_specs=[pl.BlockSpec(memory_space=pltpu.SMEM), hbm, hbm, hbm],
        out_specs=vmem,
        scratch_shapes=scratch,
        compiler_params=pltpu.CompilerParams(
            collective_id=0, has_side_effects=True, vmem_limit_bytes=58 * 1024 * 1024
        ),
    )(thickness, fields, level_count, old_pressure)
    shape = jax.ShapeDtypeStruct(old_pressure.shape, f32)
    return pl.pallas_call(
        functools.partial(write_out, rows),
        out_shape=(shape, shape),
        in_specs=[pl.BlockSpec(memory_space=pl.ANY)],
        out_specs=(hbm, hbm),
        scratch_shapes=[dma((2, 2))],
        compiler_params=pltpu.CompilerParams(vmem_limit_bytes=4 * 1024 * 1024),
    )(result)


def solution(mesh):
    ny, nx = mesh.shape["by"], mesh.shape["bx"]
    field = P("by", "bx")
    return jax.shard_map(
        functools.partial(shards, ny, nx),
        mesh=mesh,
        in_specs=(P(None, None, "by", "bx"), field, P(), field),
        out_specs=(field, field),
        check_vma=False,
    )
```

```python
import functools

import jax
import jax.numpy as jnp
from jax import lax
from jax.experimental import pallas as pl
from jax.experimental.pallas import tpu as pltpu
from jax.sharding import PartitionSpec as P

VISCOSITY = 0.05
IMPLICIT = 0.05
ITERS = 4
STEPS = 38
UNROLL = 19
UNROLL_SUM = 17
REACH = 3
MESH = pl.DeviceIdType.MESH

LANES = 128
SUB = 8
HALO = 8
PAD = 8


def lane_ids():
    return lax.broadcasted_iota(jnp.int32, (SUB, LANES), 1)


def roll(x, shift):
    shift = shift % LANES if isinstance(shift, int) else lax.rem(shift + 2 * LANES, LANES)
    return pltpu.roll(x, shift, axis=1)


def steps(count, unroll, body, carry=()):
    def chunk(n, carry):
        for m in range(unroll):
            carry = body(n * unroll + m, carry)
        return carry

    return lax.fori_loop(0, count // unroll, chunk, carry)


def from_east(tiles, lane, by=1):
    rolled = [None if x is None else roll(x, -by) for x in tiles]
    out = []
    for n in range(len(tiles)):
        a, b = rolled[n], rolled[(n + 1) % len(tiles)]
        a = 0.0 if a is None else a
        b = 0.0 if b is None else b
        out.append(jnp.where(lane >= LANES - by, b, a))
    return out


def from_west(tiles, lane, by=1):
    rolled = [None if x is None else roll(x, by) for x in tiles]
    out = []
    for n in range(len(tiles)):
        a, b = rolled[n], rolled[n - 1]
        a = 0.0 if a is None else a
        b = 0.0 if b is None else b
        out.append(jnp.where(lane < by, b, a))
    return out


def scalars(nu):
    half = 0.5

    def times_b(s):
        return [s[1]] + [half * (s[n + 1] + s[n - 1]) for n in range(1, len(s) - 1)]

    def coef_b(c):
        out = [None] * (len(c) + 1)

        def put(n, x):
            out[n] = x if out[n] is None else out[n] + x

        for n, x in enumerate(c):
            if n == 0:
                put(1, x)
            else:
                put(n + 1, half * x)
                put(n - 1, half * x)
        zero = jnp.zeros_like(c[0])
        return [zero if x is None else x for x in out]

    def plus(a, b):
        n = max(len(a), len(b))
        return [
            a[m] + b[m] if m < len(a) and m < len(b) else (a[m] if m < len(a) else b[m])
            for m in range(n)
        ]

    one = jnp.ones_like(nu[0])
    s_z, s_d = list(nu), list(nu)
    c_z, c_d = [one], [one]
    c_p = []
    norm = nu[0]
    for it in range(ITERS):
        b = times_b(s_d)
        s_a = [s_d[n] - b[n] for n in range(len(b))]
        b = coef_b(c_d)
        c_a = plus(c_d, [-x for x in b])
        alpha = norm / (c_d[it] * s_a[it])
        c_p = plus(c_p, [alpha * x for x in c_d])
        c_z = plus(c_z, [-(alpha * x) for x in c_a])
        if it + 1 < ITERS:
            s_z = [s_z[n] - alpha * s_a[n] for n in range(len(s_a))]
            new = c_z[it + 1] * s_z[it + 1]
            beta = new / norm
            norm = new
            s_d = [s_z[n] + beta * s_d[n] for n in range(len(s_z))]
            c_d = plus(c_z, [beta * x for x in c_d])
    return c_p, c_z


def kernel(
    dims,
    th,
    fields,
    level_count,
    old_pressure,
    ores,
    fb,
    lev,
    lp,
    pack,
    got1,
    got1d,
    terms,
    lcs,
    fr,
    ft,
    fold,
    got2y,
    got2x,
    got2d,
    c00,
    c0m,
    dm,
    dinv,
    q0,
    tk,
    mom,
    ar1,
    ar2,
    load_sem,
    field_sem,
    send1,
    recv1,
    send2,
    recv2,
    sendr,
    recvr,
    sendc,
    recvc,
):
    ny, nx, km, rows = dims
    ext = rows + 2 * HALO
    T = ext // SUB
    before = STEPS - T
    me_y, me_x = lax.axis_index("by"), lax.axis_index("bx")
    lane = lane_ids()
    sub = lax.broadcasted_iota(jnp.int32, (SUB, LANES), 0)
    zero = jnp.zeros((SUB, LANES), jnp.float32)

    def peer(dy, dx):
        return (lax.rem(me_y + dy + ny, ny), lax.rem(me_x + dx + nx, nx))

    peers = [peer(dy, 0) for dy in range(1, ny)] + [peer(0, dx) for dx in range(1, nx)]
    peers += [peer(dy, dx) for dy in (1, -1) for dx in (1, -1)]
    barrier = pltpu.get_barrier_semaphore()
    for x in peers:
        pl.semaphore_signal(barrier, inc=1, device_id=x, device_id_type=MESH)

    loads = []
    for c in range(2):
        cols = pl.ds(c * LANES, LANES)
        loads.append(pltpu.make_async_copy(level_count.at[:, cols], lev.at[c], load_sem.at[c]))
        loads.append(
            pltpu.make_async_copy(
                old_pressure.at[:, cols], lp.at[1, c, pl.ds(PAD + HALO, rows)], load_sem.at[2 + c]
            )
        )
    for x in loads:
        x.start()

    def field_copy(k, c):
        return pltpu.make_async_copy(
            fields.at[:, k, :, pl.ds(c * LANES, LANES)],
            fb.at[:, k, c, pl.ds(PAD + HALO, rows)],
            field_sem.at[k, c],
        )

    for k in range(km):
        for c in range(2):
            field_copy(k, c).start()

    for x in loads:
        x.wait()

    def pack_group(group, carry):
        mask = (lane >= 16 * group) & (lane < 16 * group + 16)
        out = []
        for pos in range(4):
            row = pl.multiple_of((pos * 8 + group) * SUB, SUB)
            at = pl.ds(PAD + HALO + row, SUB)
            count = [lev[c, pl.ds(row, SUB), :].astype(jnp.float32) for c in range(2)]
            for c in range(2):
                lp[0, c, at, :] = count[c]
            east = jnp.where(lane >= 120, count[1], roll(lp[1, 1, at, :], -8))
            west = jnp.where(lane < 8, count[0], roll(lp[1, 0, at, :], 8))
            out.append(jnp.where(mask, roll(east, 16 * group + 16), carry[2 * pos]))
            out.append(jnp.where(mask, roll(west, 16 * group), carry[2 * pos + 1]))
        return tuple(out)

    packed = steps(8, 8, pack_group, (zero,) * 8)
    for side in range(2):
        for pos in range(4):
            pack[side, pl.ds(pos * SUB, SUB), :] = packed[2 * pos + side]
    pl.semaphore_wait(barrier, len(peers))

    def remote(src, dst, send, recv, n, target):
        return pltpu.make_async_remote_copy(
            src_ref=src,
            dst_ref=dst,
            send_sem=send.at[n],
            recv_sem=recv.at[n],
            device_id=target,
            device_id_type=MESH,
        )

    low, high = PAD + HALO, PAD + HALO + rows - SUB
    tiles01 = pl.ds(0, 2)
    first = [
        remote(lp.at[:, tiles01, pl.ds(high, SUB)], lp.at[:, tiles01, pl.ds(PAD, SUB)], send1, recv1, 0, peer(1, 0)),
        remote(lp.at[:, tiles01, pl.ds(low, SUB)], lp.at[:, tiles01, pl.ds(high + SUB, SUB)], send1, recv1, 1, peer(-1, 0)),
        remote(pack.at[0], got1.at[0], send1, recv1, 2, peer(0, 1)),
        remote(pack.at[1], got1.at[1], send1, recv1, 3, peer(0, -1)),
        remote(pack.at[0, pl.ds(24, SUB)], got1d.at[0], send1, recv1, 4, peer(1, 1)),
        remote(pack.at[1, pl.ds(24, SUB)], got1d.at[1], send1, recv1, 5, peer(1, -1)),
        remote(pack.at[0, pl.ds(0, SUB)], got1d.at[2], send1, recv1, 6, peer(-1, 1)),
        remote(pack.at[1, pl.ds(0, SUB)], got1d.at[3], send1, recv1, 7, peer(-1, -1)),
    ]
    for x in first:
        x.start()

    def clear(k, carry):
        for f in range(3):
            for c in range(2):
                for r in (0, 8, rows + 16, rows + 24):
                    fb[f, k, c, pl.ds(r, SUB), :] = zero
        return carry

    lax.fori_loop(0, km, clear, 0)
    for n in range(2):
        for c in range(3):
            lp[n, c, pl.ds(0, SUB), :] = zero
            lp[n, c, pl.ds(ext + PAD, SUB), :] = zero

    for c in range(3):
        for r in range(T, T + 2):
            fr[c, pl.ds(r * SUB, SUB), :] = zero

    def clear_sum(t, carry):
        for c in range(3):
            tk[0, t, c] = zero
        return carry

    steps(T, 2, clear_sum, 0)

    def clear_terms(n, carry):
        for m in range(2 * REACH):
            for c in range(2):
                terms[0, n, m, c] = zero
        return carry

    steps(STEPS, 2, clear_terms, 0)

    def row_of(t):
        return pl.ds(t + PAD, SUB, stride=T)

    def level(k, carry):
        for c in range(2):
            field_copy(k, c).wait()
        scale = th[k] * (-0.5 * VISCOSITY)
        scale_u = 2.0 * scale
        scale_p = (0.5 / VISCOSITY) * scale

        def load(f, t):
            return [fb[f, k, c, row_of(t), :] for c in range(2)]

        def row_step(n, carry):
            t = n - before
            u0, u1, a0, a1, v0, v1, e0, e1, p0, p1, p2, p3 = carry
            u2, p4 = load(0, t + 2), load(2, t + 2)
            north, south = load(1, t + 3), load(1, t + 1)
            out = [[] for _ in carry]
            for c in range(2):
                u2_ = u2[c] * scale_u
                p4_ = p4[c] * scale_p
                v2 = (north[c] - south[c]) * scale
                a2 = (u2_ + u0[c]) - 4.0 * u1[c]
                e2 = (v2 + v0[c]) - 4.0 * v1[c]
                b = v0[c] + p2[c]
                d = 4.0 * e1[c]
                odd = u0[c] + ((a2 + a0[c]) - 4.0 * a1[c])
                here = ((e2 + e0[c]) + (p4_ + p0[c])) - 4.0 * (e1[c] + p2[c]) + (v0[c] + v0[c])
                for m, term in enumerate([u0[c], b - a1[c], d - odd, here, d + odd, b + a1[c]]):
                    terms[k + 1, n, m, c] = terms[k, n, m, c] + term
                row = (u1[c], u2_, a1[c], a2, v1[c], v2, e1[c], e2, p1[c], p2[c], p3[c], p4_)
                for x, y in zip(out, row):
                    x.append(y)
            return tuple(out)

        steps(STEPS, UNROLL, row_step, ([zero] * 2,) * 12)
        return carry

    lax.fori_loop(0, km, level, 0)

    for x in first:
        x.wait_recv()

    def unpack(n, shift_west, shift_east):
        def place(at, west_side, east_side, group):
            west = roll(west_side, shift_west - 16 * group)
            east = roll(east_side, shift_east - 16 * group)
            lp[n, 2, at, :] = jnp.where(lane < 64, east, west)

        def unpack_group(group, carry):
            for pos in range(4):
                row = pl.ds(pos * SUB, SUB)
                at = pl.ds(low + pl.multiple_of((pos * 8 + group) * SUB, SUB), SUB)
                place(at, got1[0, row, :], got1[1, row, :], group)
            return carry

        steps(8, 8, unpack_group, 0)
        place(pl.ds(PAD, SUB), got1d[0], got1d[1], 7)
        place(pl.ds(high + SUB, SUB), got1d[2], got1d[3], 0)

    unpack(0, 112, 0)

    def shift_counts(group, carry):
        words = []
        for c in range(3):
            word = None
            for r in range(7):
                count = lp[0, c, row_of(group * 7 + r), :].astype(jnp.int32)
                word = count if r == 0 else word | (count << (4 * r))
            words.append(word)
        for m in range(-REACH, REACH + 1):
            moved = words
            if m > 0:
                moved = from_west(words, lane, m)
            elif m < 0:
                moved = from_east(words, lane, -m)
            for c in range(2):
                for r in range(7):
                    lcs[group * 7 + r, m + REACH, c] = (moved[c] >> (4 * r)) & 15
        return carry

    steps(-(-T // 7), 5, shift_counts, 0)

    def to_rows(t, carry):
        tiles = []
        for m in range(2 * REACH + 1):
            sums = []
            for c in range(2):
                count = lcs[t, m, c]
                total = 0.0
                for k in range(km):
                    total = jnp.where(count > k, terms[k + 1, t + before, m % (2 * REACH), c], total)
                sums.append(total)
            tiles.append(sums + [None])
        total = [tiles[REACH][0], tiles[REACH][1], 0.0]
        for m in range(1, REACH + 1):
            e = from_east(tiles[REACH + m], lane, m)
            o = from_west(tiles[REACH - m], lane, m)
            for c in range(3):
                both = e[c] - o[c] if m == 3 else e[c] + o[c]
                total[c] = total[c] + (both if m == 2 else 0.5 * both)
        for c in range(3):
            fr[c, pl.ds(t, SUB, stride=T), :] = total[c]
        return carry

    steps(T, UNROLL_SUM, to_rows, 0)

    def fold_group(group, carry):
        mask = (lane >= 8 * group) & (lane < 8 * group + 8)
        out = []
        for pos in range(3):
            at = pl.ds(pl.multiple_of((pos * 12 + group) * SUB, SUB), SUB)
            east = roll(jnp.where(lane < 64, fr[2, at, :], fr[1, at, :]), 4 + 8 * group)
            west = roll(jnp.where(lane < 64, fr[0, at, :], fr[2, at, :]), 4 + 8 * group)
            out.append(jnp.where(mask, east, carry[2 * pos]))
            out.append(jnp.where(mask, west, carry[2 * pos + 1]))
        return tuple(out)

    folded = steps(12, 12, fold_group, (zero,) * 6)
    for side in range(2):
        for pos in range(3):
            fold[side, pl.ds(pos * SUB, SUB), :] = folded[2 * pos + side]
    second = [
        remote(fr.at[:, pl.ds(ext - 16, 16)], got2y.at[0], send2, recv2, 0, peer(1, 0)),
        remote(fr.at[:, pl.ds(0, 16)], got2y.at[1], send2, recv2, 1, peer(-1, 0)),
        remote(fold.at[0], got2x.at[0], send2, recv2, 2, peer(0, 1)),
        remote(fold.at[1], got2x.at[1], send2, recv2, 3, peer(0, -1)),
        remote(fold.at[0, pl.ds(16, SUB)], got2d.at[0], send2, recv2, 4, peer(1, 1)),
        remote(fold.at[1, pl.ds(16, SUB)], got2d.at[1], send2, recv2, 5, peer(1, -1)),
        remote(fold.at[0, pl.ds(0, SUB)], got2d.at[2], send2, recv2, 6, peer(-1, 1)),
        remote(fold.at[1, pl.ds(0, SUB)], got2d.at[3], send2, recv2, 7, peer(-1, -1)),
    ]
    for x in second:
        x.start()
    unpack(1, 120, -8)
    for x in first:
        x.wait_send()

    def depth_of(t):
        out = []
        for c in range(3):
            count = lp[0, c, row_of(t), :]
            total = jnp.where(count > 0.0, th[0], 0.0)
            for k in range(1, km):
                total = total + jnp.where(count > float(k), th[k], 0.0)
            out.append(total)
        return out

    def guess_of(t):
        return [jnp.where(lp[0, c, row_of(t), :] > 0.0, lp[1, c, row_of(t), :], 0.0) for c in range(3)]

    def coefficient_step(n, carry):
        t = n - 1
        depth0, mid0, west0, down0, down1, k0, guess0 = carry
        depth1 = depth_of(t + 1)
        low2 = [jnp.minimum(depth0[c], depth1[c]) for c in range(3)]
        e = from_east(low2, lane)
        mid1 = [0.5 * jnp.minimum(low2[c], e[c]) for c in range(3)]
        west1 = from_west(mid1, lane)
        guess1 = guess_of(t)
        e, o = from_east(guess1, lane), from_west(guess1, lane)
        down2 = [mid1[c] * e[c] + west1[c] * o[c] for c in range(3)]
        k1 = [(mid1[c] + mid0[c]) + (west1[c] + west0[c]) for c in range(3)]
        outside = ((sub == 0) & (t - 1 < HALO)) | ((sub == SUB - 1) & (t - 1 >= T - HALO))
        for c in range(3):
            c00[n, c] = mid1[c]
            c0m[n, c] = west1[c]
            up = mid0[c] * e[c] + west0[c] * o[c]
            diagonal = IMPLICIT + k0[c]
            dinv[n, c] = 1.0 / diagonal
            q0[n, c] = (up + down0[c]) - k0[c] * guess0[c]
            if c < 2:
                dm[n, c] = jnp.where(outside, 0.0, diagonal)
        return depth1, mid1, west1, down1, down2, k1, guess1

    steps(T + 2, 4, coefficient_step, (depth_of(-1),) + ([zero] * 3,) * 6)

    for x in second:
        x.wait_recv()

    def gather_group(group, carry):
        for pos in range(3):
            at = pl.ds(pl.multiple_of((pos * 12 + group) * SUB, SUB), SUB)
            row = pl.ds(pos * SUB, SUB)
            east = roll(got2x[0, row, :], -(4 + 8 * group))
            west = roll(got2x[1, row, :], -(4 + 8 * group))
            ft[0, at, :] = fr[0, at, :] + jnp.where(lane < 4, east, 0.0)
            ft[1, at, :] = fr[1, at, :] + jnp.where(lane >= 124, west, 0.0)
            ft[2, at, :] = fr[2, at, :] + jnp.where(lane < 4, west, jnp.where(lane >= 124, east, 0.0))
        return carry

    steps(12, 12, gather_group, 0)
    for n in range(2):
        for side in range(2):
            row = pl.ds(n * SUB, SUB)
            at = pl.ds((T - 2 + n if side else n) * SUB, SUB)
            shift = -(4 + 8 * (n if side else 8 + n))
            east = roll(got2d[2 * side], shift)
            west = roll(got2d[2 * side + 1], shift)
            ft[0, at, :] += got2y[side, 0, row, :] + jnp.where(lane < 4, east, 0.0)
            ft[1, at, :] += got2y[side, 1, row, :] + jnp.where(lane >= 124, west, 0.0)
            ft[2, at, :] += got2y[side, 2, row, :] + jnp.where(
                lane < 4, west, jnp.where(lane >= 124, east, 0.0)
            )

    def residual_step(t, carry):
        out = []
        for c in range(3):
            force = ft[c, pl.ds(t, SUB, stride=T), :]
            wet = lp[0, c, row_of(t), :] > 0.0
            z = (jnp.where(wet, force, 0.0) + q0[t + 2, c]) * dinv[t + 2, c]
            tk[1, t, c] = z
            if c < 2:
                out.append(carry[c] + (dm[t + 2, c] * z) * z)
        return tuple(out)

    acc = steps(T, 17, residual_step, (zero, zero))
    mom[0] = acc[0] + acc[1]

    def power(k, carry):
        factor = jnp.where(k == 0, 1.0, 2.0)

        def products(t):
            w = [tk[k + 1, t, c] for c in range(3)]
            e, o = from_east(w, lane), from_west(w, lane)
            dn = [c00[t + 1, c] * e[c] + c0m[t + 1, c] * o[c] for c in range(3)]
            up_ = [c00[t, c] * e[c] + c0m[t, c] * o[c] for c in range(3)]
            return w, dn, up_

        w_of, dn_of, up_of = {}, {}, {}
        w_of[T - 1], dn_of[T - 1], up_of[T - 1] = products(T - 1)
        dn_of[-1] = [pltpu.roll(x, 1, axis=0) for x in dn_of[T - 1]]
        w_of[0], dn_of[0], up_of[0] = products(0)
        up_of[T] = [pltpu.roll(x, SUB - 1, axis=0) for x in up_of[0]]
        odd, even = [zero, zero], [zero, zero]
        for t in range(T):
            if t + 1 < T - 1:
                w_of[t + 1], dn_of[t + 1], up_of[t + 1] = products(t + 1)
            for c in range(3):
                y = up_of[t + 1][c] + dn_of[t - 1][c]
                z = factor * (dinv[t + 2, c] * y) - tk[k, t, c]
                tk[k + 2, t, c] = z
                if c < 2:
                    dz = dm[t + 2, c] * z
                    odd[c] = odd[c] + dz * w_of[t][c]
                    even[c] = even[c] + dz * z
            dn_of.pop(t - 1), up_of.pop(t, None), w_of.pop(t)
        mom[2 * k + 1] = odd[0] + odd[1]
        mom[2 * k + 2] = even[0] + even[1]
        return carry

    lax.fori_loop(0, ITERS, power, 0)

    part = zero
    for n in range(2 * ITERS):
        part = jnp.where(sub == n, jnp.sum(mom[n], axis=0, keepdims=True), part)
    for by in (64, 32, 16):
        part = part + roll(part, by)
    part = jnp.sum(jnp.where(lane // 16 == sub, part, 0.0), axis=0, keepdims=True)
    ar1[me_y] = part
    col_sum = [
        remote(ar1.at[me_y], ar1.at[me_y], sendr, recvr, o, peer(o, 0)) for o in range(1, ny)
    ]
    for x in col_sum:
        x.start()
    for x in second:
        x.wait_send()
    for x in col_sum:
        x.wait_recv()
    part = sum_all(ar1, ny)
    ar2[me_x] = part
    row_sum = [
        remote(ar2.at[me_x], ar2.at[me_x], sendc, recvc, o, peer(0, o)) for o in range(1, nx)
    ]
    for x in row_sum:
        x.start()
    for x in col_sum:
        x.wait_send()
    for x in row_sum:
        x.wait_recv()
    whole = sum_all(ar2, nx)
    for by in (8, 4, 2, 1):
        whole = whole + pltpu.roll(whole, LANES - by, axis=1)
    raw = [jnp.broadcast_to(whole[:, 16 * n : 16 * n + 1], (SUB, LANES)) for n in range(2 * ITERS)]
    nu = [raw[0], raw[1]]
    for n in range(2, 2 * ITERS):
        nu.append(2.0 * raw[n] - nu[n % 2])
    c_p, c_z = scalars(nu)

    def output_step(t, carry):
        for c in range(2):
            z = [tk[m + 1, t, c] for m in range(ITERS + 1)]
            wet = lp[0, c, row_of(t), :] > 0.0
            value = jnp.where(wet, lp[1, c, row_of(t), :], 0.0)
            for m in range(ITERS):
                value = value + c_p[m] * z[m]
            ores[0, c, pl.ds(t, SUB, stride=T), :] = value
            value = c_z[0] * z[0]
            for m in range(1, ITERS + 1):
                value = value + c_z[m] * z[m]
            ores[1, c, pl.ds(t, SUB, stride=T), :] = dm[t + 2, c] * value
        return carry

    steps(T, 17, output_step, 0)
    for x in row_sum:
        x.wait_send()


def write_out(rows, ores, out_p, out_r, sem):
    stores = [
        pltpu.make_async_copy(
            ores.at[n, c, pl.ds(HALO, rows)], out.at[:, pl.ds(c * LANES, LANES)], sem.at[n, c]
        )
        for n, out in ((0, out_p), (1, out_r))
        for c in range(2)
    ]
    for x in stores:
        x.start()
    for x in stores:
        x.wait()


def sum_all(ref, count):
    parts = [ref[n] for n in range(count)]
    while len(parts) > 1:
        parts = [parts[n] + parts[n + 1] for n in range(0, len(parts), 2)]
    return parts[0]


def shards(ny, nx, fields, level_count, thickness, old_pressure):
    km, rows = fields.shape[1], fields.shape[2]
    ext = rows + 2 * HALO
    T = ext // SUB
    f32 = jnp.float32
    dma = pltpu.SemaphoreType.DMA
    vreg = (SUB, LANES)
    scratch = [
        pltpu.VMEM((3, km, 2, ext + 2 * PAD, LANES), f32),
        pltpu.VMEM((2, rows, LANES), jnp.int32),
        pltpu.VMEM((2, 3, ext + 2 * PAD, LANES), f32),
        pltpu.VMEM((2, 32, LANES), f32),
        pltpu.VMEM((2, 32, LANES), f32),
        pltpu.VMEM((4,) + vreg, f32),
        pltpu.VMEM((km + 1, STEPS, 2 * REACH, 2) + vreg, f32),
        pltpu.VMEM((T + 1, 2 * REACH + 1, 2) + vreg, jnp.int32),
        pltpu.VMEM((3, ext + 2 * SUB, LANES), f32),
        pltpu.VMEM((3, ext + 2 * SUB, LANES), f32),
        pltpu.VMEM((2, 24, LANES), f32),
        pltpu.VMEM((2, 3, 16, LANES), f32),
        pltpu.VMEM((2, 24, LANES), f32),
        pltpu.VMEM((4,) + vreg, f32),
        pltpu.VMEM((T + 2, 3) + vreg, f32),
        pltpu.VMEM((T + 2, 3) + vreg, f32),
        pltpu.VMEM((T + 2, 2) + vreg, f32),
        pltpu.VMEM((T + 2, 3) + vreg, f32),
        pltpu.VMEM((T + 2, 3) + vreg, f32),
        pltpu.VMEM((ITERS + 2, T, 3) + vreg, f32),
        pltpu.VMEM((2 * ITERS + 1,) + vreg, f32),
        pltpu.VMEM((ny, 1, LANES), f32),
        pltpu.VMEM((nx, 1, LANES), f32),
        dma((4,)),
        dma((km, 2)),
        dma((8,)),
        dma((8,)),
        dma((8,)),
        dma((8,)),
        dma((ny,)),
        dma((ny,)),
        dma((nx,)),
        dma((nx,)),
    ]
    hbm = pl.BlockSpec(memory_space=pltpu.HBM)
    vmem = pl.BlockSpec(memory_space=pltpu.VMEM)
    result = pl.pallas_call(
        functools.partial(kernel, (ny, nx, km, rows)),
        out_shape=pltpu.VMEM((2, 2, ext, LANES), f32),
        in_specs=[pl.BlockSpec(memory_space=pltpu.SMEM), hbm, hbm, hbm],
        out_specs=vmem,
        scratch_shapes=scratch,
        compiler_params=pltpu.CompilerParams(
            collective_id=0, has_side_effects=True, vmem_limit_bytes=58 * 1024 * 1024
        ),
    )(thickness, fields, level_count, old_pressure)
    shape = jax.ShapeDtypeStruct(old_pressure.shape, f32)
    return pl.pallas_call(
        functools.partial(write_out, rows),
        out_shape=(shape, shape),
        in_specs=[pl.BlockSpec(memory_space=pl.ANY)],
        out_specs=(hbm, hbm),
        scratch_shapes=[dma((2, 2))],
        compiler_params=pltpu.CompilerParams(vmem_limit_bytes=4 * 1024 * 1024),
    )(result)


def solution(mesh):
    ny, nx = mesh.shape["by"], mesh.shape["bx"]
    field = P("by", "bx")
    return jax.shard_map(
        functools.partial(shards, ny, nx),
        mesh=mesh,
        in_specs=(P(None, None, "by", "bx"), field, P(), field),
        out_specs=(field, field),
        check_vma=False,
    )
```

```python
import functools

import jax
import jax.numpy as jnp
from jax import lax
from jax.experimental import pallas as pl
from jax.experimental.pallas import tpu as pltpu
from jax.sharding import PartitionSpec as P

VISCOSITY = 0.05
IMPLICIT = 0.05
ITERS = 4
STEPS = 38
UNROLL = 19
UNROLL_SUM = 34
REACH = 3
MESH = pl.DeviceIdType.MESH

LANES = 128
SUB = 8
HALO = 8
PAD = 8


def lane_ids():
    return lax.broadcasted_iota(jnp.int32, (SUB, LANES), 1)


def roll(x, shift):
    shift = shift % LANES if isinstance(shift, int) else lax.rem(shift + 2 * LANES, LANES)
    return pltpu.roll(x, shift, axis=1)


def steps(count, unroll, body, carry=()):
    def chunk(n, carry):
        for m in range(unroll):
            carry = body(n * unroll + m, carry)
        return carry

    return lax.fori_loop(0, count // unroll, chunk, carry)


def from_east(tiles, lane, by=1):
    rolled = [None if x is None else roll(x, -by) for x in tiles]
    out = []
    for n in range(len(tiles)):
        a, b = rolled[n], rolled[(n + 1) % len(tiles)]
        a = 0.0 if a is None else a
        b = 0.0 if b is None else b
        out.append(jnp.where(lane >= LANES - by, b, a))
    return out


def from_west(tiles, lane, by=1):
    rolled = [None if x is None else roll(x, by) for x in tiles]
    out = []
    for n in range(len(tiles)):
        a, b = rolled[n], rolled[n - 1]
        a = 0.0 if a is None else a
        b = 0.0 if b is None else b
        out.append(jnp.where(lane < by, b, a))
    return out


def scalars(nu):
    half = 0.5

    def times_b(s):
        return [s[1]] + [half * (s[n + 1] + s[n - 1]) for n in range(1, len(s) - 1)]

    def coef_b(c):
        out = [None] * (len(c) + 1)

        def put(n, x):
            out[n] = x if out[n] is None else out[n] + x

        for n, x in enumerate(c):
            if n == 0:
                put(1, x)
            else:
                put(n + 1, half * x)
                put(n - 1, half * x)
        zero = jnp.zeros_like(c[0])
        return [zero if x is None else x for x in out]

    def plus(a, b):
        n = max(len(a), len(b))
        return [
            a[m] + b[m] if m < len(a) and m < len(b) else (a[m] if m < len(a) else b[m])
            for m in range(n)
        ]

    one = jnp.ones_like(nu[0])
    s_z, s_d = list(nu), list(nu)
    c_z, c_d = [one], [one]
    c_p = []
    norm = nu[0]
    for it in range(ITERS):
        b = times_b(s_d)
        s_a = [s_d[n] - b[n] for n in range(len(b))]
        b = coef_b(c_d)
        c_a = plus(c_d, [-x for x in b])
        alpha = norm / (c_d[it] * s_a[it])
        c_p = plus(c_p, [alpha * x for x in c_d])
        c_z = plus(c_z, [-(alpha * x) for x in c_a])
        if it + 1 < ITERS:
            s_z = [s_z[n] - alpha * s_a[n] for n in range(len(s_a))]
            new = c_z[it + 1] * s_z[it + 1]
            beta = new / norm
            norm = new
            s_d = [s_z[n] + beta * s_d[n] for n in range(len(s_z))]
            c_d = plus(c_z, [beta * x for x in c_d])
    return c_p, c_z


def kernel(
    dims,
    th,
    fields,
    level_count,
    old_pressure,
    ores,
    fb,
    lev,
    lp,
    pack,
    got1,
    got1d,
    terms,
    lcs,
    fr,
    ft,
    fold,
    got2y,
    got2x,
    got2d,
    c00,
    c0m,
    dm,
    dinv,
    q0,
    tk,
    mom,
    ar1,
    ar2,
    load_sem,
    field_sem,
    send1,
    recv1,
    send2,
    recv2,
    sendr,
    recvr,
    sendc,
    recvc,
):
    ny, nx, km, rows = dims
    ext = rows + 2 * HALO
    T = ext // SUB
    before = STEPS - T
    me_y, me_x = lax.axis_index("by"), lax.axis_index("bx")
    lane = lane_ids()
    sub = lax.broadcasted_iota(jnp.int32, (SUB, LANES), 0)
    zero = jnp.zeros((SUB, LANES), jnp.float32)

    def peer(dy, dx):
        return (lax.rem(me_y + dy + ny, ny), lax.rem(me_x + dx + nx, nx))

    peers = [peer(dy, 0) for dy in range(1, ny)] + [peer(0, dx) for dx in range(1, nx)]
    peers += [peer(dy, dx) for dy in (1, -1) for dx in (1, -1)]
    barrier = pltpu.get_barrier_semaphore()
    for x in peers:
        pl.semaphore_signal(barrier, inc=1, device_id=x, device_id_type=MESH)

    loads = []
    for c in range(2):
        cols = pl.ds(c * LANES, LANES)
        loads.append(pltpu.make_async_copy(level_count.at[:, cols], lev.at[c], load_sem.at[c]))
        loads.append(
            pltpu.make_async_copy(
                old_pressure.at[:, cols], lp.at[1, c, pl.ds(PAD + HALO, rows)], load_sem.at[2 + c]
            )
        )
    for x in loads:
        x.start()

    def field_copy(k, c):
        return pltpu.make_async_copy(
            fields.at[:, k, :, pl.ds(c * LANES, LANES)],
            fb.at[:, k, c, pl.ds(PAD + HALO, rows)],
            field_sem.at[k, c],
        )

    for k in range(km):
        for c in range(2):
            field_copy(k, c).start()

    for x in loads:
        x.wait()

    def pack_group(group, carry):
        mask = (lane >= 16 * group) & (lane < 16 * group + 16)
        out = []
        for pos in range(4):
            row = pl.multiple_of((pos * 8 + group) * SUB, SUB)
            at = pl.ds(PAD + HALO + row, SUB)
            count = [lev[c, pl.ds(row, SUB), :].astype(jnp.float32) for c in range(2)]
            for c in range(2):
                lp[0, c, at, :] = count[c]
            east = jnp.where(lane >= 120, count[1], roll(lp[1, 1, at, :], -8))
            west = jnp.where(lane < 8, count[0], roll(lp[1, 0, at, :], 8))
            out.append(jnp.where(mask, roll(east, 16 * group + 16), carry[2 * pos]))
            out.append(jnp.where(mask, roll(west, 16 * group), carry[2 * pos + 1]))
        return tuple(out)

    packed = steps(8, 8, pack_group, (zero,) * 8)
    for side in range(2):
        for pos in range(4):
            pack[side, pl.ds(pos * SUB, SUB), :] = packed[2 * pos + side]
    pl.semaphore_wait(barrier, len(peers))

    def remote(src, dst, send, recv, n, target):
        return pltpu.make_async_remote_copy(
            src_ref=src,
            dst_ref=dst,
            send_sem=send.at[n],
            recv_sem=recv.at[n],
            device_id=target,
            device_id_type=MESH,
        )

    low, high = PAD + HALO, PAD + HALO + rows - SUB
    tiles01 = pl.ds(0, 2)
    first = [
        remote(lp.at[:, tiles01, pl.ds(high, SUB)], lp.at[:, tiles01, pl.ds(PAD, SUB)], send1, recv1, 0, peer(1, 0)),
        remote(lp.at[:, tiles01, pl.ds(low, SUB)], lp.at[:, tiles01, pl.ds(high + SUB, SUB)], send1, recv1, 1, peer(-1, 0)),
        remote(pack.at[0], got1.at[0], send1, recv1, 2, peer(0, 1)),
        remote(pack.at[1], got1.at[1], send1, recv1, 3, peer(0, -1)),
        remote(pack.at[0, pl.ds(24, SUB)], got1d.at[0], send1, recv1, 4, peer(1, 1)),
        remote(pack.at[1, pl.ds(24, SUB)], got1d.at[1], send1, recv1, 5, peer(1, -1)),
        remote(pack.at[0, pl.ds(0, SUB)], got1d.at[2], send1, recv1, 6, peer(-1, 1)),
        remote(pack.at[1, pl.ds(0, SUB)], got1d.at[3], send1, recv1, 7, peer(-1, -1)),
    ]
    for x in first:
        x.start()

    def clear(k, carry):
        for f in range(3):
            for c in range(2):
                for r in (0, 8, rows + 16, rows + 24):
                    fb[f, k, c, pl.ds(r, SUB), :] = zero
        return carry

    lax.fori_loop(0, km, clear, 0)
    for n in range(2):
        for c in range(3):
            lp[n, c, pl.ds(0, SUB), :] = zero
            lp[n, c, pl.ds(ext + PAD, SUB), :] = zero

    for c in range(3):
        for r in range(T, T + 2):
            fr[c, pl.ds(r * SUB, SUB), :] = zero

    def clear_sum(t, carry):
        for c in range(3):
            tk[0, t, c] = zero
        return carry

    steps(T, 2, clear_sum, 0)

    def clear_terms(n, carry):
        for m in range(2 * REACH):
            for c in range(2):
                terms[0, n, m, c] = zero
        return carry

    steps(STEPS, 2, clear_terms, 0)

    def row_of(t):
        return pl.ds(t + PAD, SUB, stride=T)

    def level(k, carry):
        for c in range(2):
            field_copy(k, c).wait()
        scale = th[k] * (-0.5 * VISCOSITY)
        scale_u = 2.0 * scale
        scale_p = (0.5 / VISCOSITY) * scale

        def load(f, t):
            return [fb[f, k, c, row_of(t), :] for c in range(2)]

        def row_step(n, carry):
            t = n - before
            u0, u1, a0, a1, v0, v1, e0, e1, p0, p1, p2, p3 = carry
            u2, p4 = load(0, t + 2), load(2, t + 2)
            north, south = load(1, t + 3), load(1, t + 1)
            out = [[] for _ in carry]
            for c in range(2):
                u2_ = u2[c] * scale_u
                p4_ = p4[c] * scale_p
                v2 = (north[c] - south[c]) * scale
                a2 = (u2_ + u0[c]) - 4.0 * u1[c]
                e2 = (v2 + v0[c]) - 4.0 * v1[c]
                b = v0[c] + p2[c]
                d = 4.0 * e1[c]
                odd = u0[c] + ((a2 + a0[c]) - 4.0 * a1[c])
                here = ((e2 + e0[c]) + (p4_ + p0[c])) - 4.0 * (e1[c] + p2[c]) + (v0[c] + v0[c])
                for m, term in enumerate([u0[c], b - a1[c], d - odd, here, d + odd, b + a1[c]]):
                    terms[k + 1, n, m, c] = terms[k, n, m, c] + term
                row = (u1[c], u2_, a1[c], a2, v1[c], v2, e1[c], e2, p1[c], p2[c], p3[c], p4_)
                for x, y in zip(out, row):
                    x.append(y)
            return tuple(out)

        steps(STEPS, UNROLL, row_step, ([zero] * 2,) * 12)
        return carry

    lax.fori_loop(0, km, level, 0)

    for x in first:
        x.wait_recv()

    def unpack(n, shift_west, shift_east):
        def place(at, west_side, east_side, group):
            west = roll(west_side, shift_west - 16 * group)
            east = roll(east_side, shift_east - 16 * group)
            lp[n, 2, at, :] = jnp.where(lane < 64, east, west)

        def unpack_group(group, carry):
            for pos in range(4):
                row = pl.ds(pos * SUB, SUB)
                at = pl.ds(low + pl.multiple_of((pos * 8 + group) * SUB, SUB), SUB)
                place(at, got1[0, row, :], got1[1, row, :], group)
            return carry

        steps(8, 8, unpack_group, 0)
        place(pl.ds(PAD, SUB), got1d[0], got1d[1], 7)
        place(pl.ds(high + SUB, SUB), got1d[2], got1d[3], 0)

    unpack(0, 112, 0)

    def shift_counts(group, carry):
        words = []
        for c in range(3):
            word = None
            for r in range(7):
                count = lp[0, c, row_of(group * 7 + r), :].astype(jnp.int32)
                word = count if r == 0 else word | (count << (4 * r))
            words.append(word)
        for m in range(-REACH, REACH + 1):
            moved = words
            if m > 0:
                moved = from_west(words, lane, m)
            elif m < 0:
                moved = from_east(words, lane, -m)
            for c in range(2):
                for r in range(7):
                    lcs[group * 7 + r, m + REACH, c] = (moved[c] >> (4 * r)) & 15
        return carry

    steps(-(-T // 7), 5, shift_counts, 0)

    def to_rows(t, carry):
        tiles = []
        for m in range(2 * REACH + 1):
            sums = []
            for c in range(2):
                count = lcs[t, m, c]
                total = 0.0
                for k in range(km):
                    total = jnp.where(count > k, terms[k + 1, t + before, m % (2 * REACH), c], total)
                sums.append(total)
            tiles.append(sums + [None])
        total = [tiles[REACH][0], tiles[REACH][1], 0.0]
        for m in range(1, REACH + 1):
            e = from_east(tiles[REACH + m], lane, m)
            o = from_west(tiles[REACH - m], lane, m)
            for c in range(3):
                both = e[c] - o[c] if m == 3 else e[c] + o[c]
                total[c] = total[c] + (both if m == 2 else 0.5 * both)
        for c in range(3):
            fr[c, pl.ds(t, SUB, stride=T), :] = total[c]
        return carry

    steps(T, UNROLL_SUM, to_rows, 0)

    def fold_group(group, carry):
        mask = (lane >= 8 * group) & (lane < 8 * group + 8)
        out = []
        for pos in range(3):
            at = pl.ds(pl.multiple_of((pos * 12 + group) * SUB, SUB), SUB)
            east = roll(jnp.where(lane < 64, fr[2, at, :], fr[1, at, :]), 4 + 8 * group)
            west = roll(jnp.where(lane < 64, fr[0, at, :], fr[2, at, :]), 4 + 8 * group)
            out.append(jnp.where(mask, east, carry[2 * pos]))
            out.append(jnp.where(mask, west, carry[2 * pos + 1]))
        return tuple(out)

    folded = steps(12, 12, fold_group, (zero,) * 6)
    for side in range(2):
        for pos in range(3):
            fold[side, pl.ds(pos * SUB, SUB), :] = folded[2 * pos + side]
    second = [
        remote(fr.at[:, pl.ds(ext - 16, 16)], got2y.at[0], send2, recv2, 0, peer(1, 0)),
        remote(fr.at[:, pl.ds(0, 16)], got2y.at[1], send2, recv2, 1, peer(-1, 0)),
        remote(fold.at[0], got2x.at[0], send2, recv2, 2, peer(0, 1)),
        remote(fold.at[1], got2x.at[1], send2, recv2, 3, peer(0, -1)),
        remote(fold.at[0, pl.ds(16, SUB)], got2d.at[0], send2, recv2, 4, peer(1, 1)),
        remote(fold.at[1, pl.ds(16, SUB)], got2d.at[1], send2, recv2, 5, peer(1, -1)),
        remote(fold.at[0, pl.ds(0, SUB)], got2d.at[2], send2, recv2, 6, peer(-1, 1)),
        remote(fold.at[1, pl.ds(0, SUB)], got2d.at[3], send2, recv2, 7, peer(-1, -1)),
    ]
    for x in second:
        x.start()
    unpack(1, 120, -8)
    for x in first:
        x.wait_send()

    def depth_of(t):
        out = []
        for c in range(3):
            count = lp[0, c, row_of(t), :]
            total = jnp.where(count > 0.0, th[0], 0.0)
            for k in range(1, km):
                total = total + jnp.where(count > float(k), th[k], 0.0)
            out.append(total)
        return out

    def guess_of(t):
        return [jnp.where(lp[0, c, row_of(t), :] > 0.0, lp[1, c, row_of(t), :], 0.0) for c in range(3)]

    def coefficient_step(n, carry):
        t = n - 1
        depth0, mid0, west0, down0, down1, k0, guess0 = carry
        depth1 = depth_of(t + 1)
        low2 = [jnp.minimum(depth0[c], depth1[c]) for c in range(3)]
        e = from_east(low2, lane)
        mid1 = [0.5 * jnp.minimum(low2[c], e[c]) for c in range(3)]
        west1 = from_west(mid1, lane)
        guess1 = guess_of(t)
        e, o = from_east(guess1, lane), from_west(guess1, lane)
        down2 = [mid1[c] * e[c] + west1[c] * o[c] for c in range(3)]
        k1 = [(mid1[c] + mid0[c]) + (west1[c] + west0[c]) for c in range(3)]
        outside = ((sub == 0) & (t - 1 < HALO)) | ((sub == SUB - 1) & (t - 1 >= T - HALO))
        for c in range(3):
            c00[n, c] = mid1[c]
            c0m[n, c] = west1[c]
            up = mid0[c] * e[c] + west0[c] * o[c]
            diagonal = IMPLICIT + k0[c]
            dinv[n, c] = 1.0 / diagonal
            q0[n, c] = (up + down0[c]) - k0[c] * guess0[c]
            if c < 2:
                dm[n, c] = jnp.where(outside, 0.0, diagonal)
        return depth1, mid1, west1, down1, down2, k1, guess1

    steps(T + 2, 12, coefficient_step, (depth_of(-1),) + ([zero] * 3,) * 6)

    for x in second:
        x.wait_recv()

    def gather_group(group, carry):
        for pos in range(3):
            at = pl.ds(pl.multiple_of((pos * 12 + group) * SUB, SUB), SUB)
            row = pl.ds(pos * SUB, SUB)
            east = roll(got2x[0, row, :], -(4 + 8 * group))
            west = roll(got2x[1, row, :], -(4 + 8 * group))
            ft[0, at, :] = fr[0, at, :] + jnp.where(lane < 4, east, 0.0)
            ft[1, at, :] = fr[1, at, :] + jnp.where(lane >= 124, west, 0.0)
            ft[2, at, :] = fr[2, at, :] + jnp.where(lane < 4, west, jnp.where(lane >= 124, east, 0.0))
        return carry

    steps(12, 12, gather_group, 0)
    for n in range(2):
        for side in range(2):
            row = pl.ds(n * SUB, SUB)
            at = pl.ds((T - 2 + n if side else n) * SUB, SUB)
            shift = -(4 + 8 * (n if side else 8 + n))
            east = roll(got2d[2 * side], shift)
            west = roll(got2d[2 * side + 1], shift)
            ft[0, at, :] += got2y[side, 0, row, :] + jnp.where(lane < 4, east, 0.0)
            ft[1, at, :] += got2y[side, 1, row, :] + jnp.where(lane >= 124, west, 0.0)
            ft[2, at, :] += got2y[side, 2, row, :] + jnp.where(
                lane < 4, west, jnp.where(lane >= 124, east, 0.0)
            )

    def residual_step(t, carry):
        out = []
        for c in range(3):
            force = ft[c, pl.ds(t, SUB, stride=T), :]
            wet = lp[0, c, row_of(t), :] > 0.0
            z = (jnp.where(wet, force, 0.0) + q0[t + 2, c]) * dinv[t + 2, c]
            tk[1, t, c] = z
            if c < 2:
                out.append(carry[c] + (dm[t + 2, c] * z) * z)
        return tuple(out)

    acc = steps(T, 17, residual_step, (zero, zero))
    mom[0] = acc[0] + acc[1]

    def power(k, carry):
        factor = jnp.where(k == 0, 1.0, 2.0)

        def products(t):
            w = [tk[k + 1, t, c] for c in range(3)]
            e, o = from_east(w, lane), from_west(w, lane)
            dn = [c00[t + 1, c] * e[c] + c0m[t + 1, c] * o[c] for c in range(3)]
            up_ = [c00[t, c] * e[c] + c0m[t, c] * o[c] for c in range(3)]
            return w, dn, up_

        w_of, dn_of, up_of = {}, {}, {}
        w_of[T - 1], dn_of[T - 1], up_of[T - 1] = products(T - 1)
        dn_of[-1] = [pltpu.roll(x, 1, axis=0) for x in dn_of[T - 1]]
        w_of[0], dn_of[0], up_of[0] = products(0)
        up_of[T] = [pltpu.roll(x, SUB - 1, axis=0) for x in up_of[0]]
        odd, even = [zero, zero], [zero, zero]
        for t in range(T):
            if t + 1 < T - 1:
                w_of[t + 1], dn_of[t + 1], up_of[t + 1] = products(t + 1)
            for c in range(3):
                y = up_of[t + 1][c] + dn_of[t - 1][c]
                z = factor * (dinv[t + 2, c] * y) - tk[k, t, c]
                tk[k + 2, t, c] = z
                if c < 2:
                    dz = dm[t + 2, c] * z
                    odd[c] = odd[c] + dz * w_of[t][c]
                    even[c] = even[c] + dz * z
            dn_of.pop(t - 1), up_of.pop(t, None), w_of.pop(t)
        mom[2 * k + 1] = odd[0] + odd[1]
        mom[2 * k + 2] = even[0] + even[1]
        return carry

    lax.fori_loop(0, ITERS, power, 0)

    part = zero
    for n in range(2 * ITERS):
        part = jnp.where(sub == n, jnp.sum(mom[n], axis=0, keepdims=True), part)
    for by in (64, 32, 16):
        part = part + roll(part, by)
    part = jnp.sum(jnp.where(lane // 16 == sub, part, 0.0), axis=0, keepdims=True)
    ar1[me_y] = part
    col_sum = [
        remote(ar1.at[me_y], ar1.at[me_y], sendr, recvr, o, peer(o, 0)) for o in range(1, ny)
    ]
    for x in col_sum:
        x.start()
    for x in second:
        x.wait_send()
    for x in col_sum:
        x.wait_recv()
    part = sum_all(ar1, ny)
    ar2[me_x] = part
    row_sum = [
        remote(ar2.at[me_x], ar2.at[me_x], sendc, recvc, o, peer(0, o)) for o in range(1, nx)
    ]
    for x in row_sum:
        x.start()
    for x in col_sum:
        x.wait_send()
    for x in row_sum:
        x.wait_recv()
    whole = sum_all(ar2, nx)
    for by in (8, 4, 2, 1):
        whole = whole + pltpu.roll(whole, LANES - by, axis=1)
    raw = [jnp.broadcast_to(whole[:, 16 * n : 16 * n + 1], (SUB, LANES)) for n in range(2 * ITERS)]
    nu = [raw[0], raw[1]]
    for n in range(2, 2 * ITERS):
        nu.append(2.0 * raw[n] - nu[n % 2])
    c_p, c_z = scalars(nu)

    def output_step(t, carry):
        for c in range(2):
            z = [tk[m + 1, t, c] for m in range(ITERS + 1)]
            wet = lp[0, c, row_of(t), :] > 0.0
            value = jnp.where(wet, lp[1, c, row_of(t), :], 0.0)
            for m in range(ITERS):
                value = value + c_p[m] * z[m]
            ores[0, c, pl.ds(t, SUB, stride=T), :] = value
            value = c_z[0] * z[0]
            for m in range(1, ITERS + 1):
                value = value + c_z[m] * z[m]
            ores[1, c, pl.ds(t, SUB, stride=T), :] = dm[t + 2, c] * value
        return carry

    steps(T, 17, output_step, 0)
    for x in row_sum:
        x.wait_send()


def write_out(rows, ores, out_p, out_r, sem):
    stores = [
        pltpu.make_async_copy(
            ores.at[n, c, pl.ds(HALO, rows)], out.at[:, pl.ds(c * LANES, LANES)], sem.at[n, c]
        )
        for n, out in ((0, out_p), (1, out_r))
        for c in range(2)
    ]
    for x in stores:
        x.start()
    for x in stores:
        x.wait()


def sum_all(ref, count):
    parts = [ref[n] for n in range(count)]
    while len(parts) > 1:
        parts = [parts[n] + parts[n + 1] for n in range(0, len(parts), 2)]
    return parts[0]


def shards(ny, nx, fields, level_count, thickness, old_pressure):
    km, rows = fields.shape[1], fields.shape[2]
    ext = rows + 2 * HALO
    T = ext // SUB
    f32 = jnp.float32
    dma = pltpu.SemaphoreType.DMA
    vreg = (SUB, LANES)
    scratch = [
        pltpu.VMEM((3, km, 2, ext + 2 * PAD, LANES), f32),
        pltpu.VMEM((2, rows, LANES), jnp.int32),
        pltpu.VMEM((2, 3, ext + 2 * PAD, LANES), f32),
        pltpu.VMEM((2, 32, LANES), f32),
        pltpu.VMEM((2, 32, LANES), f32),
        pltpu.VMEM((4,) + vreg, f32),
        pltpu.VMEM((km + 1, STEPS, 2 * REACH, 2) + vreg, f32),
        pltpu.VMEM((T + 1, 2 * REACH + 1, 2) + vreg, jnp.int32),
        pltpu.VMEM((3, ext + 2 * SUB, LANES), f32),
        pltpu.VMEM((3, ext + 2 * SUB, LANES), f32),
        pltpu.VMEM((2, 24, LANES), f32),
        pltpu.VMEM((2, 3, 16, LANES), f32),
        pltpu.VMEM((2, 24, LANES), f32),
        pltpu.VMEM((4,) + vreg, f32),
        pltpu.VMEM((T + 2, 3) + vreg, f32),
        pltpu.VMEM((T + 2, 3) + vreg, f32),
        pltpu.VMEM((T + 2, 2) + vreg, f32),
        pltpu.VMEM((T + 2, 3) + vreg, f32),
        pltpu.VMEM((T + 2, 3) + vreg, f32),
        pltpu.VMEM((ITERS + 2, T, 3) + vreg, f32),
        pltpu.VMEM((2 * ITERS + 1,) + vreg, f32),
        pltpu.VMEM((ny, 1, LANES), f32),
        pltpu.VMEM((nx, 1, LANES), f32),
        dma((4,)),
        dma((km, 2)),
        dma((8,)),
        dma((8,)),
        dma((8,)),
        dma((8,)),
        dma((ny,)),
        dma((ny,)),
        dma((nx,)),
        dma((nx,)),
    ]
    hbm = pl.BlockSpec(memory_space=pltpu.HBM)
    vmem = pl.BlockSpec(memory_space=pltpu.VMEM)
    result = pl.pallas_call(
        functools.partial(kernel, (ny, nx, km, rows)),
        out_shape=pltpu.VMEM((2, 2, ext, LANES), f32),
        in_specs=[pl.BlockSpec(memory_space=pltpu.SMEM), hbm, hbm, hbm],
        out_specs=vmem,
        scratch_shapes=scratch,
        compiler_params=pltpu.CompilerParams(
            collective_id=0, has_side_effects=True, vmem_limit_bytes=58 * 1024 * 1024
        ),
    )(thickness, fields, level_count, old_pressure)
    shape = jax.ShapeDtypeStruct(old_pressure.shape, f32)
    return pl.pallas_call(
        functools.partial(write_out, rows),
        out_shape=(shape, shape),
        in_specs=[pl.BlockSpec(memory_space=pl.ANY)],
        out_specs=(hbm, hbm),
        scratch_shapes=[dma((2, 2))],
        compiler_params=pltpu.CompilerParams(vmem_limit_bytes=4 * 1024 * 1024),
    )(result)


def solution(mesh):
    ny, nx = mesh.shape["by"], mesh.shape["bx"]
    field = P("by", "bx")
    return jax.shard_map(
        functools.partial(shards, ny, nx),
        mesh=mesh,
        in_specs=(P(None, None, "by", "bx"), field, P(), field),
        out_specs=(field, field),
        check_vma=False,
    )
```
